128 devices in a mesh: dp: 64 (over z, y, x_hi, core), cent: 2 (over x_lo).
Axes of the slice: x: 4 (x_hi: 2, x_lo: 2; x = x_hi * 2 + x_lo), y: 4, z: 4, core: 2. Of those that a mesh axis runs over, the one named last changes fastest.
Arguments:
- vectors: float32 [131072, 768], P('dp'), may hold values from -24 to 24
- centroids: float32 [4096, 768], P('cent'), may hold values from -8 to 8
- head_index: int32 [2, 512], P('cent'), may hold values from 0 to 2047, as said below
- boundary_rows: int32 [64, 2, 512], P('dp', 'cent'), may hold values from 0 to 2047, as said below
- block_owner: int32 [64, 2, 4], P('dp', 'cent'), may hold values from 0 to 1, as said below
- block_live: int32 [64, 2, 4], P('dp', 'cent'), may hold values from 49 to 128
Outputs:
- new_centroids: float32 [2, 2048, 768], P('cent', 'dp')
- second_resid: bfloat16 [64, 2, 512, 768], P('dp', 'cent')
The draws below stay inside these ranges and needn't reach their ends.
Inputs may be any that keep to these rules, and one draw needn't show every extreme that they name: `head_index`: each owner's row holds 512 distinct local indices of its 2048 centroids. `boundary_rows`: each sender lists 512 distinct rows of the 2048 vector rows of its dp index; slots past a block's live count are padding. `block_owner`: no owner appears more than 2 times among one sender's 4 blocks, and some owner appears exactly 2 times in every sender; in some dp index every sender gives one owner 2 blocks.
All inputs are finite; a program needn't handle non-finite values.
Results may differ from the reference program's by a relative error of at most 0.012.
Values may be sent and summed in bfloat16 or wider, within the bound.
A program may use at most 128 MiB of HBM per device.

```python
import jax
import jax.numpy as jnp
from jax import lax

D = 768
K = 4096
ROW_DEV = 2048
HEADS = 512
BLOCK = 128
NBLK = 4
MOSTB = 2
K_DEV = 2048
ROWS = 131072
SLOTS = 512
N_DP = 64
N_CENT = 2


def centroid_matrix(key, paired):
    drawn_rows = jnp.clip(jax.random.normal(jax.random.fold_in(key, 101), (K, D), jnp.float32), -6.0, 6.0)
    odd_rows = (jnp.arange(K) % 2 == 1).astype(jnp.float32)[:, None] * paired
    return drawn_rows * (1.0 - odd_rows)


def pick_distinct(key, whole, wanted):
    middle = jax.random.permutation(key, whole - 2)[:wanted - 2].astype(jnp.int32) + 1
    chosen = jnp.concatenate([jnp.zeros((1,), jnp.int32), middle, jnp.full((1,), whole - 1, jnp.int32)])
    return jax.random.permutation(jax.random.fold_in(key, 7), chosen)


def head_choice(key):
    key = jax.random.fold_in(key, 11)
    owners = jnp.arange(N_CENT, dtype=jnp.int32)
    return jax.vmap(lambda owner: pick_distinct(jax.random.fold_in(key, owner), K // N_CENT, HEADS))(owners)


def offset_rows(values):
    row_ids = jnp.arange(ROWS, dtype=jnp.int32)
    moved = (row_ids % 8 == 3).astype(jnp.float32)[:, None]
    return jnp.clip(values + 8.0 * moved, -24.0, 24.0)


def draw_centroids(key, part):
    paired = 0.0
    return centroid_matrix(key, paired)


def draw_vectors(key, part):
    key = jax.random.fold_in(key, 5)
    return offset_rows(jnp.clip(jax.random.normal(key, (ROWS, D), jnp.float32), -6.0, 6.0))


def draw_head_index(key, part):
    return head_choice(key)


def draw_boundary_rows(key, part):
    key = jax.random.fold_in(key, 12)
    senders = jnp.arange(N_DP * N_CENT, dtype=jnp.int32)
    listed = jax.vmap(lambda sender: pick_distinct(jax.random.fold_in(key, sender), ROW_DEV, NBLK * BLOCK))(senders)
    return listed.reshape(N_DP, N_CENT, NBLK * BLOCK)


def draw_block_owner(key, part):
    key = jax.random.fold_in(key, 13)
    senders = N_DP * N_CENT
    first = jnp.minimum(jax.random.randint(jax.random.fold_in(key, 1), (senders,), 0, N_CENT), jax.random.randint(jax.random.fold_in(key, 2), (senders,), 0, N_CENT))
    others = (first[:, None] + 1 + jax.random.randint(jax.random.fold_in(key, 3), (senders, NBLK - MOSTB), 0, N_CENT - 1)) % N_CENT
    listed = jnp.concatenate([jnp.repeat(first[:, None], MOSTB, axis=1), others], axis=1).astype(jnp.int32)
    forced = jnp.concatenate([jnp.full((MOSTB,), N_CENT - 1, jnp.int32), jnp.zeros((NBLK - MOSTB,), jnp.int32)])
    chosen_dp = jax.random.randint(jax.random.fold_in(key, 4), (), 0, N_DP)
    sender_dp = jnp.arange(senders, dtype=jnp.int32) // N_CENT
    listed = jnp.where((sender_dp == chosen_dp)[:, None], forced[None, :], listed)
    ranking = jax.random.randint(jax.random.fold_in(key, 5), (senders, NBLK), 0, 1000000) * NBLK + jnp.arange(NBLK, dtype=jnp.int32)[None, :]
    order = jnp.argsort(ranking, axis=1, stable=True)
    listed = jnp.take_along_axis(listed, order, axis=1)
    return listed.reshape(N_DP, N_CENT, NBLK)


def draw_block_live(key, part):
    key = jax.random.fold_in(key, 14)
    lowest = 3 * BLOCK // 8 + 1
    live_rows = jax.random.randint(key, (N_DP, N_CENT, NBLK), lowest, BLOCK + 1).astype(jnp.int32)
    live_rows = live_rows.at[0, 0, 0].set(BLOCK)
    return live_rows.at[0, 0, 1].set(lowest)


def setup_inputs(seed: int = 0) -> dict:
    seeds = jax.random.split(jax.random.key(seed), 7)
    return {
        "vectors": draw_vectors(jax.random.fold_in(seeds[6], 71), 0),
        "centroids": draw_centroids(jax.random.fold_in(seeds[6], 71), 0),
        "head_index": draw_head_index(jax.random.fold_in(seeds[6], 71), 0),
        "boundary_rows": draw_boundary_rows(jax.random.fold_in(seeds[6], 71), 0),
        "block_owner": draw_block_owner(jax.random.fold_in(seeds[6], 71), 0),
        "block_live": draw_block_live(jax.random.fold_in(seeds[6], 71), 0),
    }


smoothing_divisor = 20.0


def match_rows(queries, head_rows, leading_length_power):
    query_f = queries.astype(jnp.float32)
    probe_length_power = jnp.sum(query_f * query_f, axis=1)
    pairwise_dots = lax.dot_general(queries, head_rows, (((1,), (1,)), ((), ())), preferred_element_type=jnp.float32)
    cluster_affinity = (2.0 * pairwise_dots - probe_length_power[:, None] - leading_length_power[None, :]) / smoothing_divisor
    row_top = jnp.max(cluster_affinity, axis=1, keepdims=True)
    exponent = jnp.exp(cluster_affinity - row_top)
    weights = (exponent / jnp.sum(exponent, axis=1, keepdims=True)).astype(jnp.bfloat16)
    mixture = jnp.dot(weights, head_rows, preferred_element_type=jnp.float32)
    return (query_f - mixture).astype(jnp.bfloat16)


def reference(vectors, centroids, head_index, boundary_rows, block_owner, block_live):
    quantized = lax.optimization_barrier(vectors.astype(jnp.bfloat16))
    centre_q = lax.optimization_barrier(centroids.astype(jnp.bfloat16))
    centre_f = centre_q.astype(jnp.float32)
    centre_length_power = jnp.sum(centre_f * centre_f, axis=1)

    def row_block(carry, block_rows):
        centre_sums, counts = carry
        block_f = block_rows.astype(jnp.float32)
        entry_length_power = jnp.sum(block_f * block_f, axis=1)
        pairwise_dots = lax.dot_general(block_rows, centre_q, (((1,), (1,)), ((), ())), preferred_element_type=jnp.float32)
        cluster_affinity = (2.0 * pairwise_dots - entry_length_power[:, None] - centre_length_power[None, :]) / smoothing_divisor
        row_top = jnp.max(cluster_affinity, axis=1, keepdims=True)
        exponent = jnp.exp(cluster_affinity - row_top)
        weights = (exponent / jnp.sum(exponent, axis=1, keepdims=True)).astype(jnp.bfloat16)
        centre_sums = centre_sums + lax.dot_general(weights, block_rows, (((0,), (0,)), ((), ())), preferred_element_type=jnp.float32)
        counts = counts + jnp.sum(weights.astype(jnp.float32), axis=0)
        return (centre_sums, counts), None

    start_sums = (jnp.zeros((K, D), jnp.float32), jnp.zeros((K,), jnp.float32))
    (centre_sums, counts), _ = lax.scan(row_block, start_sums, quantized.reshape(N_DP, ROW_DEV, D))
    updated = (centre_sums + centroids) / (counts + 1.0)[:, None]
    new_centroids = updated.reshape(N_CENT, K_DEV, D)

    block_total = N_DP * N_CENT * NBLK
    flat_rows = boundary_rows.reshape(block_total, BLOCK)
    flat_owner = block_owner.reshape(block_total)
    flat_live = block_live.reshape(block_total)
    sender_base = (jnp.arange(block_total, dtype=jnp.int32) // (N_CENT * NBLK)) * ROW_DEV

    def one_block(packed):
        row_ids, owner, live_rows, base_row = packed
        queries = jnp.take(quantized, base_row + row_ids, axis=0)
        local_heads = lax.dynamic_index_in_dim(head_index, owner, 0, keepdims=False)
        head_ids = owner * K_DEV + local_heads
        head_rows = jnp.take(centre_q, head_ids, axis=0)
        leading_length_power = jnp.take(centre_length_power, head_ids, axis=0)
        residual = match_rows(queries, head_rows, leading_length_power)
        keep_mask = jnp.arange(BLOCK, dtype=jnp.int32) < live_rows
        return jnp.where(keep_mask[:, None], residual, jnp.zeros_like(residual))

    second = lax.map(one_block, (flat_rows, flat_owner, flat_live, sender_base))
    second_resid = second.reshape(N_DP, N_CENT, SLOTS, D)
    return (new_centroids, second_resid)
```

```python
import math

import jax
import jax.numpy as jnp
from jax import lax
from jax.experimental import pallas as pl
from jax.experimental.pallas import tpu as pltpu
from jax.sharding import PartitionSpec as P

MESH = pl.DeviceIdType.MESH
F32 = jnp.float32
BF16 = jnp.bfloat16

D = 768
TILE = 256
NT = 8
NJ = 8
HALF = 128
ROWS = NJ * TILE
HEADS = 512

C1 = 0.1 * math.log2(math.e)
C2 = 0.05 * math.log2(math.e)

STAT = 0
HEAD = 2
TWIN = 4
RING = 8
CNT_T = 14
CNT_P = 15
CNT_S = 18
CNT_X = 21
SEC = 22
XHI = 28
N_REMOTE = 29

L_CEN = 0
L_VEC = 8
L_OLD = 16
L_NEW = 17
L_RES = 18
N_LOCAL = 22


def nt_dot(a, b):
    return lax.dot_general(a, b, (((1,), (1,)), ((), ())), preferred_element_type=F32)


def nn_dot(a, b):
    return jnp.dot(a, b, preferred_element_type=F32)


def kernel(
    vec, cen, hidx, brow, bown, blive,
    newc, resid,
    cst, qst, cb, qb, bias, s0, s1, e, cfin, alpha, w0, w1, cnt,
    own, tsend, trecv, rsend, rrecv, acc, xsend, xrecv, xlast,
    cs1, cs2, cs3, cr1, cr2, cr3, cr4,
    ssend, srecv, pick, hb, qs, rb, ob, old, nbuf,
    ssem, rsem, lsem,
):
    dp = lax.axis_index("dp")
    ce = lax.axis_index("cent")
    core = dp % 2
    xh = (dp // 2) % 2
    y = (dp // 4) % 4
    z = dp // 16
    prim = z * (1 - core) + y * core
    sec = y * (1 - core) + z * core
    pst = 16 * (1 - core) + 4 * core
    sst = 4 * (1 - core) + 16 * core

    def pdev(k):
        return (dp + ((prim + k) % 4 - prim) * pst, ce)

    def sdev(k):
        return (dp + ((sec + k) % 4 - sec) * sst, ce)

    twin = (dp + 1 - 2 * core, ce)
    xdev = (dp + 2 - 4 * xh, ce)
    side1 = (dp, 1 - ce)
    side2 = (dp + 2 - 4 * xh, 1 - ce)

    barrier = pltpu.get_barrier_semaphore()
    peers = [pdev(1), pdev(2), pdev(3), sdev(1), sdev(2), sdev(3), twin, xdev, side1, side2]
    for peer in peers:
        pl.semaphore_signal(barrier, inc=1, device_id=peer, device_id_type=MESH)

    def rcopy(i, src, dst, dev):
        return pltpu.make_async_remote_copy(
            src_ref=src, dst_ref=dst, send_sem=ssem.at[i], recv_sem=rsem.at[i],
            device_id=dev, device_id_type=MESH,
        )

    def lcopy(i, src, dst):
        return pltpu.make_async_copy(src, dst, lsem.at[i])

    cen_copies = [lcopy(L_CEN + t, cen.at[t, :, :, 0], cst.at[t]) for t in range(4)]
    cen_copies += [lcopy(L_CEN + 4 + t, cen.at[:, t, :, 1], cst.at[4 + t]) for t in range(4)]
    vec_copies = [
        lcopy(L_VEC + j, vec.at[pl.ds(j * TILE, TILE)], qst.at[j]) for j in range(NJ)
    ]
    vec_copies[0].start()
    for t in range(NT):
        cen_copies[t].start()
    for j in range(1, NJ):
        vec_copies[j].start()
    old_copy = lcopy(L_OLD, cen.at[z, y, xh, core], old)
    old_copy.start()

    def load_q(j):
        lcopy(L_VEC + j, vec.at[pl.ds(j * TILE, TILE)], qst.at[j]).wait()
        qb[pl.ds(pl.multiple_of(j * TILE, TILE), TILE), :] = qst[j].astype(BF16)

    def load_c(t):
        cen_copies[t].wait()
        x = cst[t].reshape(TILE, D).astype(BF16)
        cb[t] = x
        xf = x.astype(F32)
        norm = jnp.sum(xf * xf, axis=1, keepdims=True) * C2
        bias[t] = jnp.broadcast_to(norm, (TILE, TILE))

    def score(t, qj, s_ref, top):
        s = nt_dot(cb[t], qj) * C1 - bias[t]
        s_ref[t] = s
        return jnp.maximum(top, jnp.max(s.reshape(TILE // 8, 8, TILE), axis=0))

    def expo(t, j, s_ref, top, total):
        p = jnp.exp2(s_ref[t].reshape(TILE // 8, 8, TILE) - top[None])
        e[t, :, pl.ds(pl.multiple_of(j * TILE, TILE), TILE)] = p.reshape(TILE, TILE).astype(BF16)
        return total + jnp.sum(p, axis=0)

    low = jnp.full((8, TILE), -jnp.inf, F32)
    zero = jnp.zeros((8, TILE), F32)

    def whole_max(x):
        return jnp.broadcast_to(jnp.max(x, axis=0, keepdims=True), x.shape)

    def whole_sum(x):
        return jnp.broadcast_to(jnp.sum(x, axis=0, keepdims=True), x.shape)

    def q_block(j):
        return qb[pl.ds(pl.multiple_of(j * TILE, TILE), TILE), :]

    load_q(0)
    top = low
    for t in range(NT):
        load_c(t)
        top = score(t, q_block(0), s0, top)
    top = whole_max(top)

    def both(j, s_next, s_prev, top):
        load_q(j)

        def body(t, carry):
            new_top, total = carry
            new_top = score(t, q_block(j), s_next, new_top)
            total = expo(t, j - 1, s_prev, top, total)
            return new_top, total

        new_top, total = lax.fori_loop(0, NT, body, (low, zero))
        ssend[j - 1, 0] = top
        ssend[j - 1, 1] = whole_sum(total)
        return whole_max(new_top)

    def pair(i, top):
        j = 2 * i + 1
        top = both(j, s1, s0, top)
        return both(j + 1, s0, s1, top)

    top = lax.fori_loop(0, 3, pair, top)
    top = both(7, s1, s0, top)

    pl.semaphore_wait(barrier, len(peers))
    stat1 = rcopy(STAT, ssend.at[pl.ds(0, 7)], srecv.at[pl.ds(0, 7)], side1)
    stat1.start()
    total = lax.fori_loop(0, NT, lambda t, total: expo(t, 7, s1, top, total), zero)
    ssend[7, 0] = top
    ssend[7, 1] = whole_sum(total)
    stat2 = rcopy(STAT + 1, ssend.at[pl.ds(7, 1)], srecv.at[pl.ds(7, 1)], side1)
    stat2.start()

    lane = lax.broadcasted_iota(jnp.int32, (HALF, HALF), 1)

    def unit_rows(ids, place):
        column = jnp.broadcast_to(ids.astype(F32), (HALF, HALF)).T
        for k in range(ROWS // HALF):
            yield column, k

    def pick_rows(ids, place, stored_id):
        for column, k in unit_rows(ids, place):
            hit = jnp.where(column == stored_id(k).astype(F32), 1.0, 0.0)
            pick[pl.ds(place * HALF, HALF), pl.ds(k * HALF, HALF)] = hit.astype(BF16)

    def centre_id(k):
        tile, part = k // 2, k % 2
        outer = part * 2 + lane // 64
        inner = lane % 64
        inner = (inner // 32) * 64 + inner % 32
        if tile < 4:
            return tile * 512 + outer * 128 + inner
        return outer * 512 + (tile - 4) * 128 + 32 + inner

    for place in range(4):
        pick_rows(hidx[:, pl.ds(place * HALF, HALF)], place, centre_id)
    heads = nn_dot(pick[...], cb[...].reshape(ROWS, D))
    hb[ce] = heads.astype(BF16)
    head1 = rcopy(HEAD, hb.at[ce, pl.ds(0, 256)], hb.at[ce, pl.ds(0, 256)], side1)
    head2 = rcopy(HEAD + 1, hb.at[ce, pl.ds(256, 256)], hb.at[ce, pl.ds(256, 256)], side2)
    head1.start()
    head2.start()

    stat1.wait_recv()
    stat2.wait_recv()
    for j in range(NJ):
        m1, l1, m2, l2 = ssend[j, 0], ssend[j, 1], srecv[j, 0], srecv[j, 1]
        m = jnp.maximum(m1, m2)
        f1 = jnp.exp2(m1 - m)
        alpha[:, pl.ds(j * TILE, TILE)] = f1 / (l1 * f1 + l2 * jnp.exp2(m2 - m))

    def parts(base, place, step):
        if step == 0:
            t = base + (place + 2) % 4
            return (t, 0), (t, 1)
        if step == 1:
            return (base + (place + 1) % 4, 1), (base + (place + 3) % 4, 0)
        if step == 2:
            return (base + (place + 1) % 4, 0), (base + (place + 3) % 4, 1)
        return (base + place, 0), (base + place, 1)

    def tile_of(who, step):
        if who == 0:
            return parts((1 - core) * 4, sec, step)
        return parts(core * 4, prim, step)

    def scale(who, step, w_ref):
        for side, (t, half) in enumerate(tile_of(who, step)):
            count = jnp.zeros((HALF, HALF), F32)
            for c in range(NJ):
                x = e[t, pl.ds(half * HALF, HALF), pl.ds(c * TILE, TILE)].astype(F32)
                x = x.reshape(HALF // 8, 8, TILE) * alpha[:, pl.ds(c * TILE, TILE)][None]
                x = x.reshape(HALF, TILE)
                w_ref[pl.ds(side * HALF, HALF), pl.ds(c * TILE, TILE)] = x.astype(BF16)
                count = count + x[:, :HALF] + x[:, HALF:]
            cnt[pl.ds(t * 2 + half, 1), :] = jnp.sum(count.T, axis=0, keepdims=True)

    order = [(who, step) for step in range(4) for who in range(2)]
    w_refs = (w0, w1)
    twins = [rcopy(TWIN + s, tsend.at[s], trecv.at[s], twin) for s in range(4)]
    rings = [
        [rcopy(RING + 2 * s + k, rsend.at[s, k], rrecv.at[s, k], pdev((1, 3)[k])) for k in range(2)]
        for s in range(3)
    ]

    def ring_send(s):
        twins[s].wait_recv()
        for k in range(2):
            x = own[s, pl.ds(k * HALF, HALF)] + trecv[s, pl.ds(k * HALF, HALF)].astype(F32)
            if s == 2:
                rings[0][k].wait_recv()
                x = x + rrecv[0, k].astype(F32)
            rsend[s, k] = x.astype(BF16)
            rings[s][k].start()

    cnt_t = rcopy(CNT_T, cnt, cr1, twin)
    scale(0, 0, w0)
    for n, (who, step) in enumerate(order):
        out = nn_dot(w_refs[n % 2][...], qb[...])
        if n + 1 < len(order):
            scale(*order[n + 1], w_refs[(n + 1) % 2])
        if who == 0:
            tsend[step] = out.astype(BF16)
            twins[step].start()
            if step >= 1:
                ring_send(step - 1)
            if step == 3:
                cnt_t.start()
        else:
            own[step] = out

    cnt_t.wait_recv()
    cs1[...] = cnt[...] + cr1[...]
    cnt_p = [rcopy(CNT_P + k, cs1, cr2.at[k], pdev(k + 1)) for k in range(3)]
    for c in cnt_p:
        c.start()

    owner = [bown[0, b] for b in range(4)]
    slot = []
    for b in range(4):
        earlier = jnp.int32(0)
        for other in range(b):
            earlier = earlier + jnp.where(owner[other] == owner[b], 1, 0)
        slot.append(owner[b] * 2 + earlier)
    for place in range(4):
        ids = jnp.zeros((1, HALF), jnp.int32)
        for b in range(4):
            here = jnp.where(slot[b] == place, 1, 0)
            ids = ids + brow[:, pl.ds(b * HALF, HALF)] * here
        pick_rows(ids, place, lambda k: lane + k * HALF)
    qs[...] = nn_dot(pick[...], qb[...]).astype(BF16)

    twins[3].wait_recv()
    for s in (1, 2):
        for k in range(2):
            rings[s][k].wait_recv()
    for half in range(2):
        x = own[3, pl.ds(half * HALF, HALF)] + trecv[3, pl.ds(half * HALF, HALF)].astype(F32)
        x = x + rrecv[2 - half, 0].astype(F32) + rrecv[1 + half, 1].astype(F32)
        acc[pl.ds(half * 2, 2)] = x.reshape(2, 2, 32, D)

    secs = [
        [rcopy(SEC + 2 * m + k, xsend.at[m, k], xrecv.at[m, k], sdev((1, 3)[k])) for k in range(2)]
        for m in range(3)
    ]
    across, up, down = (sec + 2) % 4, (sec + 1) % 4, (sec + 3) % 4
    for m, k, chunk, part in ((0, 0, across, 0), (0, 1, across, 1), (1, 0, up, 1), (1, 1, down, 0)):
        xsend[m, k] = acc[chunk, part].astype(BF16)
        secs[m][k].start()

    for c in cnt_p:
        c.wait_recv()
    cs2[...] = cs1[...] + cr2[0] + cr2[1] + cr2[2]
    cnt_s = [rcopy(CNT_S + k, cs2, cr3.at[k], sdev(k + 1)) for k in range(3)]
    for c in cnt_s:
        c.start()

    def match(o):
        h = hb[o]
        hf = h.astype(F32)
        sq = hf * hf
        part = sq[:, :128]
        for c in range(1, D // 128):
            part = part + sq[:, c * 128:(c + 1) * 128]
        norm = jnp.concatenate(
            [jnp.sum(part[i * 128:(i + 1) * 128].T, axis=0, keepdims=True) for i in range(HEADS // 128)],
            axis=1,
        )
        q = qs[pl.ds(o * TILE, TILE), :]
        s = nt_dot(q, h) * C1 - norm * C2
        p = jnp.exp2(s - jnp.max(s, axis=1, keepdims=True))
        weights = (p / jnp.sum(p, axis=1, keepdims=True)).astype(BF16)
        r = (q.astype(F32) - nn_dot(weights, h)).astype(BF16)
        rb[pl.ds(o * 2, 2)] = r.reshape(2, HALF, D)

    head1.wait_recv()
    head2.wait_recv()
    match(0)

    for k in range(2):
        secs[0][k].wait_recv()
        chunk, part = ((up, 0), (down, 1))[k]
        xsend[2, k] = (acc[chunk, part] + xrecv[0, k].astype(F32)).astype(BF16)
        secs[2][k].start()

    match(1)

    for m in (1, 2):
        for k in range(2):
            secs[m][k].wait_recv()
    for part in range(2):
        acc[sec, part] = (
            acc[sec, part] + xrecv[2 - part, 0].astype(F32) + xrecv[1 + part, 1].astype(F32)
        )
    xlast[0] = acc[sec, 1 - xh].astype(BF16)
    last = rcopy(XHI, xlast.at[0], xlast.at[1], xdev)
    last.start()
    for c in cnt_s:
        c.wait_recv()
    cs3[...] = cs2[...] + cr3[0] + cr3[1] + cr3[2]
    cnt_x = rcopy(CNT_X, cs3, cr4, xdev)
    cnt_x.start()

    row = lax.broadcasted_iota(jnp.int32, (HALF, D), 0)
    res_copies = []
    for b in range(4):
        x = rb[slot[b]]
        ob[b] = jnp.where(row < blive[0, b], x, jnp.zeros_like(x))
        res_copies.append(lcopy(L_RES + b, ob.at[b], resid.at[pl.ds(b * HALF, HALF)]))
        res_copies[b].start()

    old_copy.wait()
    last.wait_recv()
    cnt_x.wait_recv()
    cfin[...] = cs3[...] + cr4[...]
    place = core * 1024 + prim * 256 + sec * 64 + xh * 32
    counts = jnp.broadcast_to(cfin[pl.ds(place // HALF, 1), :], (32, HALF))
    at = lax.broadcasted_iota(jnp.int32, (32, HALF), 0) + place % HALF
    hit = lax.broadcasted_iota(jnp.int32, (32, HALF), 1) == at
    count = jnp.sum(jnp.where(hit, counts, 0.0), axis=1, keepdims=True)
    total = acc[sec, xh] + xlast[1].astype(F32) + old[...]
    nbuf[...] = total / (count + 1.0)
    new_copy = lcopy(L_NEW, nbuf, newc)
    new_copy.start()

    for c in [stat1, stat2, head1, head2, cnt_t, last, cnt_x]:
        c.wait_send()
    for c in twins + cnt_p + cnt_s:
        c.wait_send()
    for group in rings + secs:
        for c in group:
            c.wait_send()
    for c in res_copies:
        c.wait()
    new_copy.wait()


def per_device(vectors, centroids, head_index, boundary_rows, block_owner, block_live):
    any_spec = pl.BlockSpec(memory_space=pl.ANY)
    vmem = pl.BlockSpec(memory_space=pltpu.VMEM)
    smem = pl.BlockSpec(memory_space=pltpu.SMEM)
    scratch = [
        pltpu.VMEM((NT, 4, 2, 32, D), F32),
        pltpu.VMEM((NJ, TILE, D), F32),
        pltpu.VMEM((NT, TILE, D), BF16),
        pltpu.VMEM((ROWS, D), BF16),
        pltpu.VMEM((NT, TILE, TILE), F32),
        pltpu.VMEM((NT, TILE, TILE), F32),
        pltpu.VMEM((NT, TILE, TILE), F32),
        pltpu.VMEM((NT, TILE, ROWS), BF16),
        pltpu.VMEM((16, HALF), F32),
        pltpu.VMEM((8, ROWS), F32),
        pltpu.VMEM((TILE, ROWS), BF16),
        pltpu.VMEM((TILE, ROWS), BF16),
        pltpu.VMEM((16, HALF), F32),
        pltpu.VMEM((4, TILE, D), F32),
        pltpu.VMEM((4, TILE, D), BF16),
        pltpu.VMEM((4, TILE, D), BF16),
        pltpu.VMEM((3, 2, HALF, D), BF16),
        pltpu.VMEM((3, 2, HALF, D), BF16),
        pltpu.VMEM((4, 2, 32, D), F32),
        pltpu.VMEM((3, 2, 32, D), BF16),
        pltpu.VMEM((3, 2, 32, D), BF16),
        pltpu.VMEM((2, 32, D), BF16),
        pltpu.VMEM((16, HALF), F32),
        pltpu.VMEM((16, HALF), F32),
        pltpu.VMEM((16, HALF), F32),
        pltpu.VMEM((16, HALF), F32),
        pltpu.VMEM((3, 16, HALF), F32),
        pltpu.VMEM((3, 16, HALF), F32),
        pltpu.VMEM((16, HALF), F32),
        pltpu.VMEM((NJ, 2, 8, TILE), F32),
        pltpu.VMEM((NJ, 2, 8, TILE), F32),
        pltpu.VMEM((HEADS, ROWS), BF16),
        pltpu.VMEM((2, HEADS, D), BF16),
        pltpu.VMEM((HEADS, D), BF16),
        pltpu.VMEM((4, HALF, D), BF16),
        pltpu.VMEM((4, HALF, D), BF16),
        pltpu.VMEM((32, D), F32),
        pltpu.VMEM((32, D), F32),
        pltpu.SemaphoreType.DMA((N_REMOTE,)),
        pltpu.SemaphoreType.DMA((N_REMOTE,)),
        pltpu.SemaphoreType.DMA((N_LOCAL,)),
    ]
    new, resid = pl.pallas_call(
        kernel,
        out_shape=(
            jax.ShapeDtypeStruct((32, D), F32),
            jax.ShapeDtypeStruct((HEADS, D), BF16),
        ),
        in_specs=[any_spec, any_spec, vmem, vmem, smem, smem],
        out_specs=(any_spec, any_spec),
        scratch_shapes=scratch,
        compiler_params=pltpu.CompilerParams(
            collective_id=0, has_side_effects=True, vmem_limit_bytes=60 * 1024 * 1024
        ),
    )(
        vectors,
        centroids.reshape(4, 4, 2, 2, 32, D),
        head_index,
        boundary_rows.reshape(1, HEADS),
        block_owner.reshape(1, 4),
        block_live.reshape(1, 4),
    )
    return new[None], resid[None, None]


def solution(mesh):
    in_specs = (
        P("dp", None),
        P("cent", None),
        P("cent", None),
        P("dp", "cent", None),
        P("dp", "cent", None),
        P("dp", "cent", None),
    )
    out_specs = (P("cent", "dp", None), P("dp", "cent", None, None))
    return jax.shard_map(
        per_device, mesh=mesh, in_specs=in_specs, out_specs=out_specs, check_vma=False
    )
```

```python
import math

import jax
import jax.numpy as jnp
from jax import lax
from jax.experimental import pallas as pl
from jax.experimental.pallas import tpu as pltpu
from jax.sharding import PartitionSpec as P

MESH = pl.DeviceIdType.MESH
F32 = jnp.float32
BF16 = jnp.bfloat16

D = 768
TILE = 256
NT = 8
NJ = 8
HALF = 128
ROWS = NJ * TILE
HEADS = 512

C1 = 0.1 * math.log2(math.e)
C2 = 0.05 * math.log2(math.e)

STAT = 0
HEAD = 2
TWIN = 4
RING = 8
RING2 = 12
CNT_T = 16
CNT_P = 17
CNT_S = 20
CNT_X = 23
SEC = 24
XHI = 27
N_REMOTE = 28

L_CEN = 0
L_VEC = 8
L_OLD = 16
N_LOCAL = 17


def nt_dot(a, b):
    return lax.dot_general(a, b, (((1,), (1,)), ((), ())), preferred_element_type=F32)


def nn_dot(a, b):
    return jnp.dot(a, b, preferred_element_type=F32)


def kernel(
    vec, cen, hidx, brow, bown, blive,
    newc, resid,
    cst, qst, cb, qb, qt0, qt1, qt2, bias, s0, s1, s2, e, cfin, alpha, w0, w1, cnt,
    own, tsend, trecv, rsend, rrecv, acc, xsend, xrecv, xlast,
    cs1, cs2, cs3, cr1, cr2, cr3, cr4,
    ssend, srecv, pick, hb, qs, rb, old,
    ssem, rsem, lsem,
):
    dp = lax.axis_index("dp")
    ce = lax.axis_index("cent")
    core = dp % 2
    xh = (dp // 2) % 2
    y = (dp // 4) % 4
    z = dp // 16
    prim = z * (1 - core) + y * core
    sec = y * (1 - core) + z * core
    pst = 16 * (1 - core) + 4 * core
    sst = 4 * (1 - core) + 16 * core

    def pdev(k):
        return (dp + ((prim + k) % 4 - prim) * pst, ce)

    def sdev(k):
        return (dp + ((sec + k) % 4 - sec) * sst, ce)

    twin = (dp + 1 - 2 * core, ce)
    xdev = (dp + 2 - 4 * xh, ce)
    side1 = (dp, 1 - ce)
    side2 = (dp + 2 - 4 * xh, 1 - ce)

    barrier = pltpu.get_barrier_semaphore()
    peers = [pdev(1), pdev(2), pdev(3), sdev(1), sdev(2), sdev(3), twin, xdev, side1, side2]
    for peer in peers:
        pl.semaphore_signal(barrier, inc=1, device_id=peer, device_id_type=MESH)

    def rcopy(i, src, dst, dev):
        return pltpu.make_async_remote_copy(
            src_ref=src, dst_ref=dst, send_sem=ssem.at[i], recv_sem=rsem.at[i],
            device_id=dev, device_id_type=MESH,
        )

    def lcopy(i, src, dst):
        return pltpu.make_async_copy(src, dst, lsem.at[i])

    cen_copies = [lcopy(L_CEN + t, cen.at[t, :, :, 0], cst.at[t]) for t in range(4)]
    cen_copies += [lcopy(L_CEN + 4 + t, cen.at[:, t, :, 1], cst.at[4 + t]) for t in range(4)]
    vec_copies = [
        lcopy(L_VEC + j, vec.at[pl.ds(j * TILE, TILE)], qst.at[j]) for j in range(NJ)
    ]
    vec_copies[0].start()
    vec_copies[1].start()
    for t in range(NT):
        cen_copies[t].start()
    for j in range(2, NJ):
        vec_copies[j].start()
    old_copy = lcopy(L_OLD, cen.at[z, y, xh, core], old)
    old_copy.start()

    def load_q(j, qt_ref):
        lcopy(L_VEC + j, vec.at[pl.ds(j * TILE, TILE)], qst.at[j]).wait()
        x = qst[j].astype(BF16)
        qb[pl.ds(pl.multiple_of(j * TILE, TILE), TILE), :] = x
        qt_ref[...] = x.T

    def load_c(t):
        cen_copies[t].wait()
        x = cst[t].reshape(TILE, D).astype(BF16)
        cb[t] = x
        xf = x.astype(F32)
        norm = jnp.sum(xf * xf, axis=1, keepdims=True) * C2
        bias[t] = jnp.broadcast_to(norm, (TILE, TILE))

    def score(t, qt_ref, s_ref, top):
        s = nn_dot(cb[t], qt_ref[...]) * C1 - bias[t]
        s_ref[t] = s
        return jnp.maximum(top, jnp.max(s.reshape(TILE // 8, 8, TILE), axis=0))

    def expo(t, j, s_ref, top, total):
        p = jnp.exp2(s_ref[t].reshape(TILE // 8, 8, TILE) - top[None])
        e[t, :, pl.ds(pl.multiple_of(j * TILE, TILE), TILE)] = p.reshape(TILE, TILE).astype(BF16)
        return total + jnp.sum(p, axis=0)

    low = jnp.full((8, TILE), -jnp.inf, F32)
    zero = jnp.zeros((8, TILE), F32)

    def whole_max(x):
        return jnp.broadcast_to(jnp.max(x, axis=0, keepdims=True), x.shape)

    def whole_sum(x):
        return jnp.broadcast_to(jnp.sum(x, axis=0, keepdims=True), x.shape)

    load_q(0, qt0)
    load_q(1, qt1)
    load_c(0)
    top0, top1 = low, low
    for t in range(NT):
        if t + 1 < NT:
            load_c(t + 1)
        top0 = score(t, qt0, s0, top0)
        top1 = score(t, qt1, s1, top1)
    load_q(2, qt2)

    def put_stats(j, top, total):
        ssend[j, 0] = top
        ssend[j, 1] = whole_sum(total)

    def both(j, s_next, qt, qt_next, prevs):
        if qt_next is not None:
            load_q(j + 1, qt_next)
        new_top = low
        totals = [zero] * len(prevs)
        for t in range(NT):
            new_top = score(t, qt, s_next, new_top)
            totals = [expo(t, i, s_prev, top, total) for (i, s_prev, top), total in zip(prevs, totals)]
        for (i, _, top), total in zip(prevs, totals):
            put_stats(i, top, total)
        return whole_max(new_top)

    top = both(2, s2, qt2, qt0, [(0, s0, whole_max(top0)), (1, s1, whole_max(top1))])

    def pair(i, top):
        j = 2 * i + 3
        top = both(j, s0, qt0, qt2, [(j - 1, s2, top)])
        return both(j + 1, s2, qt2, qt0, [(j, s0, top)])

    for i in range(2):
        top = pair(i, top)
    top = both(7, s0, qt0, None, [(6, s2, top)])

    pl.semaphore_wait(barrier, len(peers))
    stat1 = rcopy(STAT, ssend.at[pl.ds(0, 7)], srecv.at[pl.ds(0, 7)], side1)
    stat1.start()
    total = zero
    for t in range(NT):
        total = expo(t, 7, s0, top, total)
    put_stats(7, top, total)
    stat2 = rcopy(STAT + 1, ssend.at[pl.ds(7, 1)], srecv.at[pl.ds(7, 1)], side1)
    stat2.start()

    lane = lax.broadcasted_iota(jnp.int32, (HALF, HALF), 1)

    def unit_rows(ids, place):
        column = jnp.broadcast_to(ids.astype(F32), (HALF, HALF)).T
        for k in range(ROWS // HALF):
            yield column, k

    def pick_rows(ids, place, stored_id):
        for column, k in unit_rows(ids, place):
            hit = jnp.where(column == stored_id(k).astype(F32), 1.0, 0.0)
            pick[pl.ds(place * HALF, HALF), pl.ds(k * HALF, HALF)] = hit.astype(BF16)

    def centre_id(k):
        tile, part = k // 2, k % 2
        outer = part * 2 + lane // 64
        inner = lane % 64
        inner = (inner // 32) * 64 + inner % 32
        if tile < 4:
            return tile * 512 + outer * 128 + inner
        return outer * 512 + (tile - 4) * 128 + 32 + inner

    for place in range(4):
        pick_rows(hidx[:, pl.ds(place * HALF, HALF)], place, centre_id)
    heads = nn_dot(pick[...], cb[...].reshape(ROWS, D))
    hb[ce] = heads.astype(BF16)
    head1 = rcopy(HEAD, hb.at[ce, pl.ds(0, 256)], hb.at[ce, pl.ds(0, 256)], side1)
    head2 = rcopy(HEAD + 1, hb.at[ce, pl.ds(256, 256)], hb.at[ce, pl.ds(256, 256)], side2)
    head1.start()
    head2.start()

    stat1.wait_recv()
    stat2.wait_recv()
    for j in range(NJ):
        m1, l1, m2, l2 = ssend[j, 0], ssend[j, 1], srecv[j, 0], srecv[j, 1]
        m = jnp.maximum(m1, m2)
        f1 = jnp.exp2(m1 - m)
        alpha[:, pl.ds(j * TILE, TILE)] = f1 / (l1 * f1 + l2 * jnp.exp2(m2 - m))

    def parts(base, place, step):
        if step == 0:
            t = base + (place + 2) % 4
            return (t, 0), (t, 1)
        if step == 1:
            return (base + (place + 1) % 4, 1), (base + (place + 3) % 4, 0)
        if step == 2:
            return (base + (place + 1) % 4, 0), (base + (place + 3) % 4, 1)
        return (base + place, 0), (base + place, 1)

    def tile_of(who, step):
        if who == 0:
            return parts((1 - core) * 4, sec, step)
        return parts(core * 4, prim, step)

    def scale(who, step, w_ref):
        for side, (t, half) in enumerate(tile_of(who, step)):
            count = jnp.zeros((HALF, HALF), F32)
            for c in range(NJ):
                x = e[t, pl.ds(half * HALF, HALF), pl.ds(c * TILE, TILE)].astype(F32)
                x = x.reshape(HALF // 8, 8, TILE) * alpha[:, pl.ds(c * TILE, TILE)][None]
                x = x.reshape(HALF, TILE)
                w_ref[pl.ds(side * HALF, HALF), pl.ds(c * TILE, TILE)] = x.astype(BF16)
                count = count + x[:, :HALF] + x[:, HALF:]
            cnt[pl.ds(t * 2 + half, 1), :] = jnp.sum(count.T, axis=0, keepdims=True)

    order = [(0, 0), (0, 1), (1, 0), (0, 2), (1, 1), (1, 2), (0, 3), (1, 3)]
    w_refs = (w0, w1)
    twins = [rcopy(TWIN + s, tsend.at[s], trecv.at[s], twin) for s in range(4)]
    rings = [
        [rcopy(RING + 2 * s + k, rsend.at[s, k], rrecv.at[s, k], pdev((1, 3)[k])) for k in range(2)]
        for s in range(2)
    ]
    lead = [sec % 2 + (1 - 2 * (sec % 2)) * (k * (sec // 2) + (1 - k) * (1 - sec // 2)) for k in range(2)]
    spots = [[pl.ds(c * 64, 64) for c in (lead[k], 1 - lead[k])] for k in range(2)]
    ring2 = [
        [
            rcopy(RING2 + 2 * k + n, rsend.at[2, k, spots[k][n]], rrecv.at[2, k, spots[k][n]], pdev((1, 3)[k]))
            for n in range(2)
        ]
        for k in range(2)
    ]

    def ring_send(s):
        twins[s].wait_recv()
        for k in range(2):
            x = own[s, pl.ds(k * HALF, HALF)] + trecv[s, pl.ds(k * HALF, HALF)].astype(F32)
            if s == 2:
                rings[0][k].wait_recv()
                x = x + rrecv[0, k].astype(F32)
            rsend[s, k] = x.astype(BF16)
            if s < 2:
                rings[s][k].start()
            else:
                ring2[k][0].start()
                ring2[k][1].start()

    cnt_t = rcopy(CNT_T, cnt, cr1, twin)
    scale(0, 0, w0)
    for n, (who, step) in enumerate(order):
        out = nn_dot(w_refs[n % 2][...], qb[...])
        if n + 1 < len(order):
            scale(*order[n + 1], w_refs[(n + 1) % 2])
        if who == 0:
            tsend[step] = out.astype(BF16)
            twins[step].start()
            if step == 3:
                cnt_t.start()
                ring_send(2)
        else:
            own[step] = out
            if step < 2:
                ring_send(step)

    cnt_t.wait_recv()
    cs1[...] = cnt[...] + cr1[...]
    cnt_p = [rcopy(CNT_P + k, cs1, cr2.at[k], pdev(k + 1)) for k in range(3)]
    for c in cnt_p:
        c.start()

    owner = [bown[0, b] for b in range(4)]
    slot = []
    for b in range(4):
        earlier = jnp.int32(0)
        for other in range(b):
            earlier = earlier + jnp.where(owner[other] == owner[b], 1, 0)
        slot.append(owner[b] * 2 + earlier)
    for place in range(4):
        ids = jnp.zeros((1, HALF), jnp.int32)
        for b in range(4):
            here = jnp.where(slot[b] == place, 1, 0)
            ids = ids + brow[:, pl.ds(b * HALF, HALF)] * here
        pick_rows(ids, place, lambda k: lane + k * HALF)
    qs[...] = nn_dot(pick[...], qb[...]).astype(BF16)

    twins[3].wait_recv()
    rings[1][0].wait_recv()
    rings[1][1].wait_recv()
    for half in range(2):
        x = own[3, pl.ds(half * HALF, HALF)] + trecv[3, pl.ds(half * HALF, HALF)].astype(F32)
        x = x + rrecv[1, 1 - half].astype(F32)
        acc[pl.ds(half * 2, 2)] = x.reshape(2, 64, D)

    def finish_chunk(chunk):
        return acc[chunk] + rrecv[2, chunk // 2, pl.ds((chunk % 2) * 64, 64)].astype(F32)

    secs = [rcopy(SEC + k, xsend.at[k], xrecv.at[k], sdev(k + 1)) for k in range(3)]

    def send_chunk(k):
        xsend[k] = finish_chunk((sec + k + 1) % 4).astype(BF16)
        secs[k].start()

    def counts_on():
        for c in cnt_p:
            c.wait_recv()
        cs2[...] = cs1[...] + cr2[0] + cr2[1] + cr2[2]
        for c in cnt_s:
            c.start()

    cnt_s = [rcopy(CNT_S + k, cs2, cr3.at[k], sdev(k + 1)) for k in range(3)]

    def match(o):
        h = hb[o]
        hf = h.astype(F32)
        sq = hf * hf
        part = sq[:, :128]
        for c in range(1, D // 128):
            part = part + sq[:, c * 128:(c + 1) * 128]
        norm = jnp.concatenate(
            [jnp.sum(part[i * 128:(i + 1) * 128].T, axis=0, keepdims=True) for i in range(HEADS // 128)],
            axis=1,
        )
        q = qs[pl.ds(o * TILE, TILE), :]
        s = nt_dot(q, h) * C1 - norm * C2
        p = jnp.exp2(s - jnp.max(s, axis=1, keepdims=True))
        weights = (p / jnp.sum(p, axis=1, keepdims=True)).astype(BF16)
        r = (q.astype(F32) - nn_dot(weights, h)).astype(BF16)
        rb[pl.ds(o * 2, 2)] = r.reshape(2, HALF, D)

    for k in range(2):
        ring2[k][0].wait_recv()
        ring2[k][1].wait_recv()
    for k in (1, 0, 2):
        send_chunk(k)
    counts_on()

    head1.wait_recv()
    head2.wait_recv()
    match(0)
    match(1)

    for c in secs:
        c.wait_recv()
    total = finish_chunk(sec) + xrecv[0].astype(F32) + xrecv[1].astype(F32) + xrecv[2].astype(F32)
    acc[sec] = total
    xlast[0] = acc[sec, pl.ds((1 - xh) * 32, 32)].astype(BF16)
    last = rcopy(XHI, xlast.at[0], xlast.at[1], xdev)
    last.start()
    for c in cnt_s:
        c.wait_recv()
    cs3[...] = cs2[...] + cr3[0] + cr3[1] + cr3[2]
    cnt_x = rcopy(CNT_X, cs3, cr4, xdev)
    cnt_x.start()

    row = lax.broadcasted_iota(jnp.int32, (HALF, D), 0)
    for b in range(4):
        x = rb[slot[b]]
        resid[pl.ds(b * HALF, HALF), :] = jnp.where(row < blive[0, b], x, jnp.zeros_like(x))

    old_copy.wait()
    last.wait_recv()
    cnt_x.wait_recv()
    cfin[...] = cs3[...] + cr4[...]
    place = core * 1024 + prim * 256 + sec * 64 + xh * 32
    counts = jnp.broadcast_to(cfin[pl.ds(place // HALF, 1), :], (32, HALF))
    at = lax.broadcasted_iota(jnp.int32, (32, HALF), 0) + place % HALF
    hit = lax.broadcasted_iota(jnp.int32, (32, HALF), 1) == at
    count = jnp.sum(jnp.where(hit, counts, 0.0), axis=1, keepdims=True)
    total = acc[sec, pl.ds(xh * 32, 32)] + xlast[1].astype(F32) + old[...]
    newc[...] = total / (count + 1.0)

    for c in [stat1, stat2, head1, head2, cnt_t, last, cnt_x]:
        c.wait_send()
    for c in twins + cnt_p + cnt_s + secs:
        c.wait_send()
    for group in rings + ring2:
        for c in group:
            c.wait_send()


def hand_over(new, resid, new_out, resid_out, sems):
    copies = [
        pltpu.make_async_copy(new, new_out, sems.at[0]),
        pltpu.make_async_copy(resid, resid_out, sems.at[1]),
    ]
    for c in copies:
        c.start()
    for c in copies:
        c.wait()


def per_device(vectors, centroids, head_index, boundary_rows, block_owner, block_live):
    any_spec = pl.BlockSpec(memory_space=pl.ANY)
    vmem = pl.BlockSpec(memory_space=pltpu.VMEM)
    smem = pl.BlockSpec(memory_space=pltpu.SMEM)
    scratch = [
        pltpu.VMEM((NT, 4, 2, 32, D), F32),
        pltpu.VMEM((NJ, TILE, D), F32),
        pltpu.VMEM((NT, TILE, D), BF16),
        pltpu.VMEM((ROWS, D), BF16),
        pltpu.VMEM((D, TILE), BF16),
        pltpu.VMEM((D, TILE), BF16),
        pltpu.VMEM((D, TILE), BF16),
        pltpu.VMEM((NT, TILE, TILE), F32),
        pltpu.VMEM((NT, TILE, TILE), F32),
        pltpu.VMEM((NT, TILE, TILE), F32),
        pltpu.VMEM((NT, TILE, TILE), F32),
        pltpu.VMEM((NT, TILE, ROWS), BF16),
        pltpu.VMEM((16, HALF), F32),
        pltpu.VMEM((8, ROWS), F32),
        pltpu.VMEM((TILE, ROWS), BF16),
        pltpu.VMEM((TILE, ROWS), BF16),
        pltpu.VMEM((16, HALF), F32),
        pltpu.VMEM((4, TILE, D), F32),
        pltpu.VMEM((4, TILE, D), BF16),
        pltpu.VMEM((4, TILE, D), BF16),
        pltpu.VMEM((3, 2, HALF, D), BF16),
        pltpu.VMEM((3, 2, HALF, D), BF16),
        pltpu.VMEM((4, 64, D), F32),
        pltpu.VMEM((3, 64, D), BF16),
        pltpu.VMEM((3, 64, D), BF16),
        pltpu.VMEM((2, 32, D), BF16),
        pltpu.VMEM((16, HALF), F32),
        pltpu.VMEM((16, HALF), F32),
        pltpu.VMEM((16, HALF), F32),
        pltpu.VMEM((16, HALF), F32),
        pltpu.VMEM((3, 16, HALF), F32),
        pltpu.VMEM((3, 16, HALF), F32),
        pltpu.VMEM((16, HALF), F32),
        pltpu.VMEM((NJ, 2, 8, TILE), F32),
        pltpu.VMEM((NJ, 2, 8, TILE), F32),
        pltpu.VMEM((HEADS, ROWS), BF16),
        pltpu.VMEM((2, HEADS, D), BF16),
        pltpu.VMEM((HEADS, D), BF16),
        pltpu.VMEM((4, HALF, D), BF16),
        pltpu.VMEM((32, D), F32),
        pltpu.SemaphoreType.DMA((N_REMOTE,)),
        pltpu.SemaphoreType.DMA((N_REMOTE,)),
        pltpu.SemaphoreType.DMA((N_LOCAL,)),
    ]
    new, resid = pl.pallas_call(
        kernel,
        out_shape=(
            pltpu.VMEM((32, D), F32),
            pltpu.VMEM((HEADS, D), BF16),
        ),
        in_specs=[any_spec, any_spec, vmem, vmem, smem, smem],
        out_specs=(vmem, vmem),
        scratch_shapes=scratch,
        compiler_params=pltpu.CompilerParams(
            collective_id=0, has_side_effects=True, vmem_limit_bytes=60 * 1024 * 1024
        ),
    )(
        vectors,
        centroids.reshape(4, 4, 2, 2, 32, D),
        head_index,
        boundary_rows.reshape(1, HEADS),
        block_owner.reshape(1, 4),
        block_live.reshape(1, 4),
    )
    new, resid = pl.pallas_call(
        hand_over,
        out_shape=(
            jax.ShapeDtypeStruct((32, D), F32),
            jax.ShapeDtypeStruct((HEADS, D), BF16),
        ),
        in_specs=[vmem, vmem],
        out_specs=(any_spec, any_spec),
        scratch_shapes=[pltpu.SemaphoreType.DMA((2,))],
    )(new, resid)
    return new[None], resid[None, None]


def solution(mesh):
    in_specs = (
        P("dp", None),
        P("cent", None),
        P("cent", None),
        P("dp", "cent", None),
        P("dp", "cent", None),
        P("dp", "cent", None),
    )
    out_specs = (P("cent", "dp", None), P("dp", "cent", None, None))
    return jax.shard_map(
        per_device, mesh=mesh, in_specs=in_specs, out_specs=out_specs, check_vma=False
    )
```

```python
import math

import jax
import jax.numpy as jnp
from jax import lax
from jax.experimental import pallas as pl
from jax.experimental.pallas import tpu as pltpu
from jax.sharding import PartitionSpec as P

MESH = pl.DeviceIdType.MESH
F32 = jnp.float32
BF16 = jnp.bfloat16

D = 768
TILE = 256
NT = 8
NJ = 8
AHEAD = 2
HALF = 128
ROWS = NJ * TILE
HEADS = 512

C1 = 0.1 * math.log2(math.e)
C2 = 0.05 * math.log2(math.e)

STAT = 0
HEAD = 2
TWIN = 4
RING = 8
RING2 = 12
CNT_T = 16
CNT_P = 17
CNT_S = 20
SEC = 27
XHI = 33
N_REMOTE = 34

L_CEN = 0
L_VEC = 8
L_OLD = 16
N_LOCAL = 17


def nt_dot(a, b):
    return lax.dot_general(a, b, (((1,), (1,)), ((), ())), preferred_element_type=F32)


def nn_dot(a, b):
    return jnp.dot(a, b, preferred_element_type=F32)


def kernel(
    vec, cen, hidx, brow, bown, blive,
    newc, resid,
    cst, qst, cb, qb, qt0, qt1, qt2, bias, s0, s1, s2, e, cfin, alpha, w0, w1, cnt,
    tsend, trecv, rsend, rrecv, acc, xsend, xrecv, xlast,
    cs1, cs2, cr1, cr2, cr3,
    ssend, srecv, pick, hb, qs, rb, old,
    ssem, rsem, lsem,
):
    dp = lax.axis_index("dp")
    ce = lax.axis_index("cent")
    core = dp % 2
    xh = (dp // 2) % 2
    y = (dp // 4) % 4
    z = dp // 16
    prim = z * (1 - core) + y * core
    sec = y * (1 - core) + z * core
    pst = 16 * (1 - core) + 4 * core
    sst = 4 * (1 - core) + 16 * core

    def pdev(k):
        return (dp + ((prim + k) % 4 - prim) * pst, ce)

    def sdev(k):
        return (dp + ((sec + k) % 4 - sec) * sst, ce)

    def sxdev(k):
        return (sdev(k)[0] + 2 - 4 * xh, ce)

    twin = (dp + 1 - 2 * core, ce)
    xdev = (dp + 2 - 4 * xh, ce)
    side1 = (dp, 1 - ce)
    side2 = (dp + 2 - 4 * xh, 1 - ce)

    barrier = pltpu.get_barrier_semaphore()
    peers = [pdev(1), pdev(2), pdev(3), sdev(1), sdev(2), sdev(3), sxdev(1), sxdev(2), sxdev(3)]
    peers += [twin, xdev, side1, side2]
    for peer in peers:
        pl.semaphore_signal(barrier, inc=1, device_id=peer, device_id_type=MESH)

    def rcopy(i, src, dst, dev):
        return pltpu.make_async_remote_copy(
            src_ref=src, dst_ref=dst, send_sem=ssem.at[i], recv_sem=rsem.at[i],
            device_id=dev, device_id_type=MESH,
        )

    def lcopy(i, src, dst):
        return pltpu.make_async_copy(src, dst, lsem.at[i])

    cen_copies = [lcopy(L_CEN + t, cen.at[t, :, :, 0], cst.at[t]) for t in range(4)]
    cen_copies += [lcopy(L_CEN + 4 + t, cen.at[:, t, :, 1], cst.at[4 + t]) for t in range(4)]
    vec_copies = [
        lcopy(L_VEC + j, vec.at[pl.ds(j * TILE, TILE)], qst.at[j]) for j in range(NJ)
    ]
    vec_copies[0].start()
    cen_copies[0].start()
    for j in range(1, AHEAD):
        vec_copies[j].start()
    for t in range(1, NT):
        cen_copies[t].start()
    for j in range(AHEAD, NJ):
        vec_copies[j].start()
    old_copy = lcopy(L_OLD, cen.at[z, y, xh, core], old)
    old_copy.start()

    def load_q(j, qt_ref):
        lcopy(L_VEC + j, vec.at[pl.ds(j * TILE, TILE)], qst.at[j]).wait()
        x = qst[j].astype(BF16)
        qb[pl.ds(pl.multiple_of(j * TILE, TILE), TILE), :] = x
        qt_ref[...] = x.T

    def load_c(t):
        cen_copies[t].wait()
        x = cst[t].reshape(TILE, D).astype(BF16)
        cb[t] = x
        xf = x.astype(F32)
        norm = jnp.sum(xf * xf, axis=1, keepdims=True) * C2
        bias[t] = jnp.broadcast_to(norm, (TILE, HALF))

    def score(t, qt_ref, s_ref, top):
        b = bias[t]
        s = nn_dot(cb[t], qt_ref[...]) * C1 - jnp.concatenate([b, b], axis=1)
        s_ref[t] = s
        return jnp.maximum(top, jnp.max(s.reshape(TILE // 8, 8, TILE), axis=0))

    def expo(t, j, s_ref, top, total):
        p = jnp.exp2(s_ref[t].reshape(TILE // 8, 8, TILE) - top[None])
        e[t, :, pl.ds(pl.multiple_of(j * TILE, TILE), TILE)] = p.reshape(TILE, TILE).astype(BF16)
        return total + jnp.sum(p, axis=0)

    low = jnp.full((8, TILE), -jnp.inf, F32)
    zero = jnp.zeros((8, TILE), F32)

    def whole_max(x):
        return jnp.broadcast_to(jnp.max(x, axis=0, keepdims=True), x.shape)

    def whole_sum(x):
        return jnp.broadcast_to(jnp.sum(x, axis=0, keepdims=True), x.shape)

    def put_stats(j, top, total):
        ssend[j, 0] = top
        ssend[j, 1] = whole_sum(total)

    load_q(0, qt0)
    load_c(0)
    top0, top1 = low, low
    for t in range(NT):
        if t == 0:
            load_q(1, qt1)
        else:
            top1 = score(t - 1, qt1, s1, top1)
        if t + 1 < NT:
            load_c(t + 1)
        top0 = score(t, qt0, s0, top0)
    load_q(2, qt2)
    top1 = score(NT - 1, qt1, s1, top1)

    def both(j, s_next, qt_ref, qt_next, prevs):
        if qt_next is not None:
            load_q(j + 1, qt_next)
        new_top = low
        totals = [zero] * len(prevs)
        for t in range(NT):
            new_top = score(t, qt_ref, s_next, new_top)
            totals = [expo(t, i, ref, top, total) for (i, ref, top), total in zip(prevs, totals)]
        for (i, _, top), total in zip(prevs, totals):
            put_stats(i, top, total)
        return whole_max(new_top)

    top = both(2, s2, qt2, qt0, [(0, s0, whole_max(top0)), (1, s1, whole_max(top1))])

    def pair(i, top):
        j = 2 * i + 3
        top = both(j, s0, qt0, qt2, [(j - 1, s2, top)])
        return both(j + 1, s2, qt2, qt0, [(j, s0, top)])

    top = lax.fori_loop(0, 2, pair, top)
    top = both(7, s0, qt0, None, [(6, s2, top)])
    s_last = s0

    pl.semaphore_wait(barrier, len(peers))
    stat1 = rcopy(STAT, ssend.at[pl.ds(0, 7)], srecv.at[pl.ds(0, 7)], side1)
    stat1.start()
    total = zero
    for t in range(NT):
        total = expo(t, 7, s_last, top, total)
    put_stats(7, top, total)
    stat2 = rcopy(STAT + 1, ssend.at[pl.ds(7, 1)], srecv.at[pl.ds(7, 1)], side1)
    stat2.start()

    lane = lax.broadcasted_iota(jnp.int32, (HALF, HALF), 1)

    def unit_rows(ids, place):
        column = jnp.broadcast_to(ids.astype(F32), (HALF, HALF)).T
        for k in range(ROWS // HALF):
            yield column, k

    def pick_rows(ids, place, stored_id):
        for column, k in unit_rows(ids, place):
            hit = jnp.where(column == stored_id(k).astype(F32), 1.0, 0.0)
            pick[pl.ds(place * HALF, HALF), pl.ds(k * HALF, HALF)] = hit.astype(BF16)

    def centre_id(k):
        tile, part = k // 2, k % 2
        outer = part * 2 + lane // 64
        inner = lane % 64
        inner = (inner // 32) * 64 + inner % 32
        if tile < 4:
            return tile * 512 + outer * 128 + inner
        return outer * 512 + (tile - 4) * 128 + 32 + inner

    for place in range(4):
        pick_rows(hidx[:, pl.ds(place * HALF, HALF)], place, centre_id)
    heads = nn_dot(pick[...], cb[...].reshape(ROWS, D))
    hb[ce] = heads.astype(BF16)
    head1 = rcopy(HEAD, hb.at[ce, pl.ds(0, 256)], hb.at[ce, pl.ds(0, 256)], side1)
    head2 = rcopy(HEAD + 1, hb.at[ce, pl.ds(256, 256)], hb.at[ce, pl.ds(256, 256)], side2)
    head1.start()
    head2.start()

    def parts(base, place, step):
        if step == 0:
            t = base + (place + 2) % 4
            return (t, 0), (t, 1)
        if step == 1:
            return (base + (place + 1) % 4, 1), (base + (place + 3) % 4, 0)
        if step == 2:
            return (base + (place + 1) % 4, 0), (base + (place + 3) % 4, 1)
        return (base + place, 0), (base + place, 1)

    def tile_of(who, step):
        if who == 0:
            return parts((1 - core) * 4, sec, step)
        return parts(core * 4, prim, step)

    def scale(who, step, w_ref, columns, counts, last):
        out = []
        for side, (t, half) in enumerate(tile_of(who, step)):
            partial = []
            for c in columns:
                x = e[t, pl.ds(half * HALF, HALF), pl.ds(c * TILE, TILE)]
                x = x.reshape(HALF // 16, 16, TILE) * alpha[:, pl.ds(c * TILE, TILE)][None]
                x = x.reshape(HALF, TILE)
                w_ref[pl.ds(side * HALF, HALF), pl.ds(c * TILE, TILE)] = x
                partial.append(x[:, :HALF] + x[:, HALF:])
            count = counts[side]
            while partial:
                some, partial = partial[:4], partial[4:]
                while len(some) > 1:
                    some = [some[0] + some[1]] + some[2:] if len(some) != 4 else [some[0] + some[1], some[2] + some[3]]
                count = count + some[0].astype(F32)
            if last:
                cnt[pl.ds(t * 2 + half, 1), :] = jnp.sum(count.T, axis=0, keepdims=True)
            out.append(count)
        return out

    none = [jnp.zeros((HALF, HALF), F32)] * 2

    def row_scale(j):
        m1, l1, m2, l2 = ssend[j, 0], ssend[j, 1], srecv[j, 0], srecv[j, 1]
        m = jnp.maximum(m1, m2)
        f1 = jnp.exp2(m1 - m)
        a = f1 / (l1 * f1 + l2 * jnp.exp2(m2 - m))
        alpha[:, pl.ds(j * TILE, TILE)] = jnp.concatenate([a, a], axis=0).astype(BF16)

    stat1.wait_recv()
    for j in range(NJ - 1):
        row_scale(j)
    first = scale(0, 0, w0, range(NJ - 1), none, False)
    stat2.wait_recv()
    row_scale(NJ - 1)
    scale(0, 0, w0, [NJ - 1], first, True)

    order = [(0, 0), (0, 1), (1, 0), (0, 2), (1, 1), (1, 2), (0, 3), (1, 3)]
    w_refs = (w0, w1)
    twins = [rcopy(TWIN + s, tsend.at[s], trecv.at[s], twin) for s in range(4)]
    rings = [
        [rcopy(RING + 2 * s + k, rsend.at[s, k], rrecv.at[s, k], pdev((1, 3)[k])) for k in range(2)]
        for s in range(2)
    ]
    lead = [sec % 2 + (1 - 2 * (sec % 2)) * (k * (sec // 2) + (1 - k) * (1 - sec // 2)) for k in range(2)]
    spots = [[pl.ds(c * 64, 64) for c in (lead[k], 1 - lead[k])] for k in range(2)]
    ring2 = [
        [
            rcopy(RING2 + 2 * k + n, rsend.at[2, k, spots[k][n]], rrecv.at[2, k, spots[k][n]], pdev((1, 3)[k]))
            for n in range(2)
        ]
        for k in range(2)
    ]

    def own(s, half):
        return cst[s, pl.ds(half * 2, 2)].reshape(HALF, D)

    def ring_send(s):
        twins[s].wait_recv()
        for k in range(2):
            x = own(s, k) + trecv[s, pl.ds(k * HALF, HALF)].astype(F32)
            if s == 2:
                rings[0][k].wait_recv()
                x = x + rrecv[0, k].astype(F32)
            rsend[s, k] = x.astype(BF16)
            if s < 2:
                rings[s][k].start()
            else:
                ring2[k][0].start()
                ring2[k][1].start()

    cnt_t = rcopy(CNT_T, cnt, cr1, twin)
    for n, (who, step) in enumerate(order):
        out = nn_dot(w_refs[n % 2][...], qb[...])
        if n + 1 < len(order):
            scale(*order[n + 1], w_refs[(n + 1) % 2], range(NJ), none, True)
        if who == 0:
            tsend[step] = out.astype(BF16)
            twins[step].start()
            if step == 3:
                cnt_t.start()
                ring_send(2)
        else:
            cst[step] = out.reshape(4, 2, 32, D)
            if step < 2:
                ring_send(step)

    cnt_t.wait_recv()
    cs1[...] = cnt[...] + cr1[...]
    cnt_p = [rcopy(CNT_P + k, cs1, cr2.at[k], pdev(k + 1)) for k in range(3)]
    for c in cnt_p:
        c.start()

    owner = [bown[0, b] for b in range(4)]
    slot = []
    for b in range(4):
        earlier = jnp.int32(0)
        for other in range(b):
            earlier = earlier + jnp.where(owner[other] == owner[b], 1, 0)
        slot.append(owner[b] * 2 + earlier)
    for place in range(4):
        ids = jnp.zeros((1, HALF), jnp.int32)
        for b in range(4):
            here = jnp.where(slot[b] == place, 1, 0)
            ids = ids + brow[:, pl.ds(b * HALF, HALF)] * here
        pick_rows(ids, place, lambda k: lane + k * HALF)
    qs[...] = nn_dot(pick[...], qb[...]).astype(BF16)

    twins[3].wait_recv()
    rings[1][0].wait_recv()
    rings[1][1].wait_recv()
    for half in range(2):
        x = own(3, half) + trecv[3, pl.ds(half * HALF, HALF)].astype(F32)
        x = x + rrecv[1, 1 - half].astype(F32)
        acc[pl.ds(half * 2, 2)] = x.reshape(2, 64, D)

    def finish_rows(chunk, part):
        got = rrecv[2, chunk // 2, pl.ds((chunk % 2) * 64 + part * 32, 32)]
        return acc[chunk, pl.ds(part * 32, 32)] + got.astype(F32)

    odd = sec % 2
    steps = [1 + 2 * odd, 2, 3 - 2 * odd]
    secs = [
        [rcopy(SEC + 2 * i + n, xsend.at[i, n], xrecv.at[i, n], sdev(k)) for n in range(2)]
        for i, k in enumerate(steps)
    ]
    sides = [1 - xh, xh]

    def send_chunks(pairings):
        for n in range(2):
            for i in pairings:
                xsend[i, n] = finish_rows((sec + steps[i]) % 4, sides[n]).astype(BF16)
                secs[i][n].start()

    def own_rows(n):
        total = finish_rows(sec, sides[n])
        for i in range(3):
            total = total + xrecv[i, n].astype(F32)
        return total

    def counts_on():
        for c in cnt_p:
            c.wait_recv()
        cs2[...] = cs1[...] + cr2[0] + cr2[1] + cr2[2]
        for c in cnt_s:
            c.start()

    group = [sdev(1), sdev(2), sdev(3), xdev, sxdev(1), sxdev(2), sxdev(3)]
    cnt_s = [rcopy(CNT_S + k, cs2, cr3.at[k], dev) for k, dev in enumerate(group)]

    def match(o):
        h = hb[o]
        hf = h.astype(F32)
        sq = hf * hf
        part = sq[:, :128]
        for c in range(1, D // 128):
            part = part + sq[:, c * 128:(c + 1) * 128]
        norm = jnp.concatenate(
            [jnp.sum(part[i * 128:(i + 1) * 128].T, axis=0, keepdims=True) for i in range(HEADS // 128)],
            axis=1,
        )
        q = qs[pl.ds(o * TILE, TILE), :]
        s = nt_dot(q, h) * C1 - norm * C2
        p = jnp.exp2(s - jnp.max(s, axis=1, keepdims=True))
        weights = (p / jnp.sum(p, axis=1, keepdims=True)).astype(BF16)
        r = (q.astype(F32) - nn_dot(weights, h)).astype(BF16)
        rb[pl.ds(o * 2, 2)] = r.reshape(2, HALF, D)

    ring2[0][0].wait_recv()
    ring2[1][0].wait_recv()
    send_chunks((1, 0))
    ring2[0][1].wait_recv()
    ring2[1][1].wait_recv()
    send_chunks((2,))
    counts_on()

    head1.wait_recv()
    head2.wait_recv()
    match(0)

    for i in range(3):
        secs[i][0].wait_recv()
    xlast[0] = own_rows(0).astype(BF16)
    last = rcopy(XHI, xlast.at[0], xlast.at[1], xdev)
    last.start()
    match(1)

    row = lax.broadcasted_iota(jnp.int32, (HALF, D), 0)
    for b in range(4):
        x = rb[slot[b]]
        resid[pl.ds(b * HALF, HALF), :] = jnp.where(row < blive[0, b], x, jnp.zeros_like(x))

    old_copy.wait()
    for i in range(3):
        secs[i][1].wait_recv()
    for c in cnt_s:
        c.wait_recv()
    counts = cs2[...]
    for k in range(7):
        counts = counts + cr3[k]
    cfin[...] = counts
    place = core * 1024 + prim * 256 + sec * 64 + xh * 32
    counts = jnp.broadcast_to(cfin[pl.ds(place // HALF, 1), :], (32, HALF))
    at = lax.broadcasted_iota(jnp.int32, (32, HALF), 0) + place % HALF
    hit = lax.broadcasted_iota(jnp.int32, (32, HALF), 1) == at
    count = jnp.sum(jnp.where(hit, counts, 0.0), axis=1, keepdims=True)
    total = own_rows(1) + old[...]
    last.wait_recv()
    newc[...] = (total + xlast[1].astype(F32)) / (count + 1.0)

    for c in [stat1, stat2, head1, head2, cnt_t, last]:
        c.wait_send()
    for c in twins + cnt_p + cnt_s:
        c.wait_send()
    for pair in rings + ring2 + secs:
        for c in pair:
            c.wait_send()


def hand_over(new, resid, new_out, resid_out, sems):
    copies = [
        pltpu.make_async_copy(new, new_out, sems.at[0]),
        pltpu.make_async_copy(resid, resid_out, sems.at[1]),
    ]
    for c in copies:
        c.start()
    for c in copies:
        c.wait()


def per_device(vectors, centroids, head_index, boundary_rows, block_owner, block_live):
    any_spec = pl.BlockSpec(memory_space=pl.ANY)
    vmem = pl.BlockSpec(memory_space=pltpu.VMEM)
    smem = pl.BlockSpec(memory_space=pltpu.SMEM)
    scratch = [
        pltpu.VMEM((NT, 4, 2, 32, D), F32),
        pltpu.VMEM((NJ, TILE, D), F32),
        pltpu.VMEM((NT, TILE, D), BF16),
        pltpu.VMEM((ROWS, D), BF16),
        pltpu.VMEM((D, TILE), BF16),
        pltpu.VMEM((D, TILE), BF16),
        pltpu.VMEM((D, TILE), BF16),
        pltpu.VMEM((NT, TILE, HALF), F32),
        pltpu.VMEM((NT, TILE, TILE), F32),
        pltpu.VMEM((NT, TILE, TILE), F32),
        pltpu.VMEM((NT, TILE, TILE), F32),
        pltpu.VMEM((NT, TILE, ROWS), BF16),
        pltpu.VMEM((16, HALF), F32),
        pltpu.VMEM((16, ROWS), BF16),
        pltpu.VMEM((TILE, ROWS), BF16),
        pltpu.VMEM((TILE, ROWS), BF16),
        pltpu.VMEM((16, HALF), F32),
        pltpu.VMEM((4, TILE, D), BF16),
        pltpu.VMEM((4, TILE, D), BF16),
        pltpu.VMEM((3, 2, HALF, D), BF16),
        pltpu.VMEM((3, 2, HALF, D), BF16),
        pltpu.VMEM((4, 64, D), F32),
        pltpu.VMEM((3, 2, 32, D), BF16),
        pltpu.VMEM((3, 2, 32, D), BF16),
        pltpu.VMEM((2, 32, D), BF16),
        pltpu.VMEM((16, HALF), F32),
        pltpu.VMEM((16, HALF), F32),
        pltpu.VMEM((16, HALF), F32),
        pltpu.VMEM((3, 16, HALF), F32),
        pltpu.VMEM((7, 16, HALF), F32),
        pltpu.VMEM((NJ, 2, 8, TILE), F32),
        pltpu.VMEM((NJ, 2, 8, TILE), F32),
        pltpu.VMEM((HEADS, ROWS), BF16),
        pltpu.VMEM((2, HEADS, D), BF16),
        pltpu.VMEM((HEADS, D), BF16),
        pltpu.VMEM((4, HALF, D), BF16),
        pltpu.VMEM((32, D), F32),
        pltpu.SemaphoreType.DMA((N_REMOTE,)),
        pltpu.SemaphoreType.DMA((N_REMOTE,)),
        pltpu.SemaphoreType.DMA((N_LOCAL,)),
    ]
    new, resid = pl.pallas_call(
        kernel,
        out_shape=(
            pltpu.VMEM((32, D), F32),
            pltpu.VMEM((HEADS, D), BF16),
        ),
        in_specs=[any_spec, any_spec, vmem, vmem, smem, smem],
        out_specs=(vmem, vmem),
        scratch_shapes=scratch,
        compiler_params=pltpu.CompilerParams(
            collective_id=0, has_side_effects=True, vmem_limit_bytes=60 * 1024 * 1024
        ),
    )(
        vectors,
        centroids.reshape(4, 4, 2, 2, 32, D),
        head_index,
        boundary_rows.reshape(1, HEADS),
        block_owner.reshape(1, 4),
        block_live.reshape(1, 4),
    )
    new, resid = pl.pallas_call(
        hand_over,
        out_shape=(
            jax.ShapeDtypeStruct((32, D), F32),
            jax.ShapeDtypeStruct((HEADS, D), BF16),
        ),
        in_specs=[vmem, vmem],
        out_specs=(any_spec, any_spec),
        scratch_shapes=[pltpu.SemaphoreType.DMA((2,))],
        compiler_params=pltpu.CompilerParams(vmem_limit_bytes=4 * 1024 * 1024),
    )(new, resid)
    return new[None], resid[None, None]


def solution(mesh):
    in_specs = (
        P("dp", None),
        P("cent", None),
        P("cent", None),
        P("dp", "cent", None),
        P("dp", "cent", None),
        P("dp", "cent", None),
    )
    out_specs = (P("cent", "dp", None), P("dp", "cent", None, None))
    return jax.shard_map(
        per_device, mesh=mesh, in_specs=in_specs, out_specs=out_specs, check_vma=False
    )
```

```python
import math

import jax
import jax.numpy as jnp
from jax import lax
from jax.experimental import pallas as pl
from jax.experimental.pallas import tpu as pltpu
from jax.sharding import PartitionSpec as P

MESH = pl.DeviceIdType.MESH
F32 = jnp.float32
BF16 = jnp.bfloat16

D = 768
TILE = 256
NT = 8
NJ = 8
AHEAD = 2
HALF = 128
ROWS = NJ * TILE
HEADS = 512

C1 = 0.1 * math.log2(math.e)
C2 = 0.05 * math.log2(math.e)

STAT = 0
HEAD = 2
TWIN = 4
RING0 = 8
RING1 = 12
RING2 = 14
CNT_T = 18
CNT_P = 19
CNT_S = 22
SEC = 29
XHI = 35
N_REMOTE = 36

L_CEN = 0
L_VEC = 8
L_OLD = 16
N_LOCAL = 17


def nt_dot(a, b):
    return lax.dot_general(a, b, (((1,), (1,)), ((), ())), preferred_element_type=F32)


def nn_dot(a, b):
    return jnp.dot(a, b, preferred_element_type=F32)


def kernel(
    vec, cen, hidx, brow, bown, blive,
    newc, resid,
    cst, qst, cb, qb, qt0, qt1, qt2, bias, s0, s1, s2, e, cfin, alpha, w0, w1, cnt,
    tsend, trecv, rsend, rrecv, acc, xsend, xrecv, xlast,
    cs1, cs2, cr1, cr2, cr3,
    ssend, srecv, pick, hb, qs, rb, old,
    ssem, rsem, lsem,
):
    dp = lax.axis_index("dp")
    ce = lax.axis_index("cent")
    core = dp % 2
    xh = (dp // 2) % 2
    y = (dp // 4) % 4
    z = dp // 16
    prim = z * (1 - core) + y * core
    sec = y * (1 - core) + z * core
    pst = 16 * (1 - core) + 4 * core
    sst = 4 * (1 - core) + 16 * core

    def pdev(k):
        return (dp + ((prim + k) % 4 - prim) * pst, ce)

    def sdev(k):
        return (dp + ((sec + k) % 4 - sec) * sst, ce)

    def sxdev(k):
        return (sdev(k)[0] + 2 - 4 * xh, ce)

    twin = (dp + 1 - 2 * core, ce)
    xdev = (dp + 2 - 4 * xh, ce)
    side1 = (dp, 1 - ce)
    side2 = (dp + 2 - 4 * xh, 1 - ce)

    barrier = pltpu.get_barrier_semaphore()
    peers = [pdev(1), pdev(2), pdev(3), sdev(1), sdev(2), sdev(3), sxdev(1), sxdev(2), sxdev(3)]
    peers += [twin, xdev, side1, side2]
    for peer in peers:
        pl.semaphore_signal(barrier, inc=1, device_id=peer, device_id_type=MESH)

    def rcopy(i, src, dst, dev):
        return pltpu.make_async_remote_copy(
            src_ref=src, dst_ref=dst, send_sem=ssem.at[i], recv_sem=rsem.at[i],
            device_id=dev, device_id_type=MESH,
        )

    def lcopy(i, src, dst):
        return pltpu.make_async_copy(src, dst, lsem.at[i])

    cen_copies = [lcopy(L_CEN + t, cen.at[t, :, :, 0], cst.at[t]) for t in range(4)]
    cen_copies += [lcopy(L_CEN + 4 + t, cen.at[:, t, :, 1], cst.at[4 + t]) for t in range(4)]
    vec_copies = [
        lcopy(L_VEC + j, vec.at[pl.ds(j * TILE, TILE)], qst.at[j]) for j in range(NJ)
    ]
    vec_copies[0].start()
    cen_copies[0].start()
    for j in range(1, AHEAD):
        vec_copies[j].start()
    for t in range(1, NT):
        cen_copies[t].start()
    for j in range(AHEAD, NJ):
        vec_copies[j].start()
    old_copy = lcopy(L_OLD, cen.at[z, y, xh, core], old)
    old_copy.start()

    def load_q(j, qt_ref):
        lcopy(L_VEC + j, vec.at[pl.ds(j * TILE, TILE)], qst.at[j]).wait()
        x = qst[j].astype(BF16)
        qb[pl.ds(pl.multiple_of(j * TILE, TILE), TILE), :] = x
        qt_ref[...] = x.T

    def load_c(t):
        cen_copies[t].wait()
        x = cst[t].reshape(TILE, D).astype(BF16)
        cb[t] = x
        xf = x.astype(F32)
        norm = jnp.sum(xf * xf, axis=1, keepdims=True) * C2
        bias[t] = jnp.broadcast_to(norm, (TILE, HALF))

    def score(t, qt_ref, s_ref, top):
        b = bias[t]
        s = nn_dot(cb[t], qt_ref[...]) * C1 - jnp.concatenate([b, b], axis=1)
        s_ref[t] = s
        return jnp.maximum(top, jnp.max(s.reshape(TILE // 8, 8, TILE), axis=0))

    def expo(t, j, s_ref, top, total):
        p = jnp.exp2(s_ref[t].reshape(TILE // 8, 8, TILE) - top[None])
        e[t, :, pl.ds(pl.multiple_of(j * TILE, TILE), TILE)] = p.reshape(TILE, TILE).astype(BF16)
        return total + jnp.sum(p, axis=0)

    low = jnp.full((8, TILE), -jnp.inf, F32)
    zero = jnp.zeros((8, TILE), F32)

    def whole_max(x):
        return jnp.broadcast_to(jnp.max(x, axis=0, keepdims=True), x.shape)

    def whole_sum(x):
        return jnp.broadcast_to(jnp.sum(x, axis=0, keepdims=True), x.shape)

    def put_stats(j, top, total):
        ssend[j, 0] = top
        ssend[j, 1] = whole_sum(total)

    load_q(0, qt0)
    load_c(0)
    top0, top1 = low, low
    for t in range(NT):
        if t == 0:
            load_q(1, qt1)
        else:
            top1 = score(t - 1, qt1, s1, top1)
        if t + 1 < NT:
            load_c(t + 1)
        top0 = score(t, qt0, s0, top0)
    load_q(2, qt2)
    top1 = score(NT - 1, qt1, s1, top1)

    def both(j, s_next, qt_ref, qt_next, prevs):
        if qt_next is not None:
            load_q(j + 1, qt_next)
        new_top = low
        totals = [zero] * len(prevs)
        for t in range(NT):
            new_top = score(t, qt_ref, s_next, new_top)
            totals = [expo(t, i, ref, top, total) for (i, ref, top), total in zip(prevs, totals)]
        for (i, _, top), total in zip(prevs, totals):
            put_stats(i, top, total)
        return whole_max(new_top)

    top = both(2, s2, qt2, qt0, [(0, s0, whole_max(top0)), (1, s1, whole_max(top1))])

    def pair(i, top):
        j = 2 * i + 3
        top = both(j, s0, qt0, qt2, [(j - 1, s2, top)])
        return both(j + 1, s2, qt2, qt0, [(j, s0, top)])

    top = lax.fori_loop(0, 2, pair, top)
    top = both(7, s0, qt0, None, [(6, s2, top)])
    s_last = s0

    pl.semaphore_wait(barrier, len(peers))
    stat1 = rcopy(STAT, ssend.at[pl.ds(0, 7)], srecv.at[pl.ds(0, 7)], side1)
    stat1.start()
    total = zero
    for t in range(NT):
        total = expo(t, 7, s_last, top, total)
    put_stats(7, top, total)
    stat2 = rcopy(STAT + 1, ssend.at[pl.ds(7, 1)], srecv.at[pl.ds(7, 1)], side1)
    stat2.start()

    lane = lax.broadcasted_iota(jnp.int32, (HALF, HALF), 1)

    def unit_rows(ids, place):
        column = jnp.broadcast_to(ids.astype(F32), (HALF, HALF)).T
        for k in range(ROWS // HALF):
            yield column, k

    def pick_rows(ids, place, stored_id):
        for column, k in unit_rows(ids, place):
            hit = jnp.where(column == stored_id(k).astype(F32), 1.0, 0.0)
            pick[pl.ds(place * HALF, HALF), pl.ds(k * HALF, HALF)] = hit.astype(BF16)

    def centre_id(k):
        tile, part = k // 2, k % 2
        outer = part * 2 + lane // 64
        inner = lane % 64
        inner = (inner // 32) * 64 + inner % 32
        if tile < 4:
            return tile * 512 + outer * 128 + inner
        return outer * 512 + (tile - 4) * 128 + 32 + inner

    for place in range(4):
        pick_rows(hidx[:, pl.ds(place * HALF, HALF)], place, centre_id)
    heads = nn_dot(pick[...], cb[...].reshape(ROWS, D))
    hb[ce] = heads.astype(BF16)
    head1 = rcopy(HEAD, hb.at[ce, pl.ds(0, 256)], hb.at[ce, pl.ds(0, 256)], side1)
    head2 = rcopy(HEAD + 1, hb.at[ce, pl.ds(256, 256)], hb.at[ce, pl.ds(256, 256)], side2)
    head1.start()
    head2.start()

    def parts(base, place, step):
        if step == 0:
            t = base + (place + 2) % 4
            return (t, 0), (t, 1)
        if step == 1:
            return (base + (place + 1) % 4, 1), (base + (place + 3) % 4, 0)
        if step == 2:
            return (base + (place + 1) % 4, 0), (base + (place + 3) % 4, 1)
        return (base + place, 0), (base + place, 1)

    def tile_of(who, step):
        if who == 0:
            return parts((1 - core) * 4, sec, step)
        return parts(core * 4, prim, step)

    def scale(who, step, w_ref, columns, counts, last):
        out = []
        for side, (t, half) in enumerate(tile_of(who, step)):
            partial = []
            for c in columns:
                x = e[t, pl.ds(half * HALF, HALF), pl.ds(c * TILE, TILE)]
                x = x.reshape(HALF // 16, 16, TILE) * alpha[:, pl.ds(c * TILE, TILE)][None]
                x = x.reshape(HALF, TILE)
                w_ref[pl.ds(side * HALF, HALF), pl.ds(c * TILE, TILE)] = x
                partial.append(x[:, :HALF] + x[:, HALF:])
            count = counts[side]
            while partial:
                some, partial = partial[:4], partial[4:]
                while len(some) > 1:
                    some = [some[0] + some[1]] + some[2:] if len(some) != 4 else [some[0] + some[1], some[2] + some[3]]
                count = count + some[0].astype(F32)
            if last:
                cnt[pl.ds(t * 2 + half, 1), :] = jnp.sum(count.T, axis=0, keepdims=True)
            out.append(count)
        return out

    none = [jnp.zeros((HALF, HALF), F32)] * 2

    def row_scale(j):
        m1, l1, m2, l2 = ssend[j, 0], ssend[j, 1], srecv[j, 0], srecv[j, 1]
        m = jnp.maximum(m1, m2)
        f1 = jnp.exp2(m1 - m)
        a = f1 / (l1 * f1 + l2 * jnp.exp2(m2 - m))
        alpha[:, pl.ds(j * TILE, TILE)] = jnp.concatenate([a, a], axis=0).astype(BF16)

    stat1.wait_recv()
    for j in range(NJ - 1):
        row_scale(j)
    first = scale(0, 0, w0, range(NJ - 1), none, False)
    stat2.wait_recv()
    row_scale(NJ - 1)
    scale(0, 0, w0, [NJ - 1], first, True)

    order = [(0, 0), (0, 1), (1, 0), (0, 2), (1, 1), (1, 2), (0, 3), (1, 3)]
    w_refs = (w0, w1)
    twins = [rcopy(TWIN + s, tsend.at[s], trecv.at[s], twin) for s in range(4)]
    lead = [sec % 2 + (1 - 2 * (sec % 2)) * (k * (sec // 2) + (1 - k) * (1 - sec // 2)) for k in range(2)]
    chunks = [(lead[k], 1 - lead[k]) for k in range(2)]
    spots = [[pl.ds(pl.multiple_of(c * 64, 64), 64) for c in chunks[k]] for k in range(2)]
    around = [pdev(1), pdev(3)]

    def ring_parts(first, s):
        return [
            [
                rcopy(first + 2 * k + n, rsend.at[s, k, spots[k][n]], rrecv.at[s, k, spots[k][n]], around[k])
                for n in range(2)
            ]
            for k in range(2)
        ]

    ring0, ring2 = ring_parts(RING0, 0), ring_parts(RING2, 2)
    ring1 = [rcopy(RING1 + k, rsend.at[1, k], rrecv.at[1, k], around[k]) for k in range(2)]

    def own(s, half):
        return cst[s, pl.ds(half * 2, 2)].reshape(HALF, D)

    def send_part(s, n):
        for k in range(2):
            c = 2 * k + chunks[k][n]
            x = cst[s, c].reshape(64, D)
            x = x + trecv[s, pl.ds(pl.multiple_of(c * 64, 64), 64)].astype(F32)
            if s == 2:
                ring0[k][n].wait_recv()
                x = x + rrecv[0, k, spots[k][n]].astype(F32)
            rsend[s, k, spots[k][n]] = x.astype(BF16)
            (ring2 if s == 2 else ring0)[k][n].start()

    def send_middle():
        for k in range(2):
            x = own(1, k) + trecv[1, pl.ds(k * HALF, HALF)].astype(F32)
            rsend[1, k] = x.astype(BF16)
            ring1[k].start()

    cnt_t = rcopy(CNT_T, cnt, cr1, twin)
    for n, (who, step) in enumerate(order):
        out = nn_dot(w_refs[n % 2][...], qb[...])
        if n + 1 < len(order):
            scale(*order[n + 1], w_refs[(n + 1) % 2], range(NJ), none, True)
        if who == 0:
            tsend[step] = out.astype(BF16)
            twins[step].start()
            if step == 3:
                cnt_t.start()
                twins[2].wait_recv()
                send_part(2, 0)
        else:
            cst[step] = out.reshape(4, 2, 32, D)
            if step == 0:
                twins[0].wait_recv()
                send_part(0, 0)
                send_part(0, 1)
            if step == 1:
                twins[1].wait_recv()
                send_middle()
            if step == 3:
                send_part(2, 1)

    cnt_t.wait_recv()
    cs1[...] = cnt[...] + cr1[...]
    cnt_p = [rcopy(CNT_P + k, cs1, cr2.at[k], pdev(k + 1)) for k in range(3)]
    for c in cnt_p:
        c.start()

    owner = [bown[0, b] for b in range(4)]
    slot = []
    for b in range(4):
        earlier = jnp.int32(0)
        for other in range(b):
            earlier = earlier + jnp.where(owner[other] == owner[b], 1, 0)
        slot.append(owner[b] * 2 + earlier)
    for place in range(4):
        ids = jnp.zeros((1, HALF), jnp.int32)
        for b in range(4):
            here = jnp.where(slot[b] == place, 1, 0)
            ids = ids + brow[:, pl.ds(b * HALF, HALF)] * here
        pick_rows(ids, place, lambda k: lane + k * HALF)
    qs[...] = nn_dot(pick[...], qb[...]).astype(BF16)

    twins[3].wait_recv()
    ring1[0].wait_recv()
    ring1[1].wait_recv()
    for half in range(2):
        x = own(3, half) + trecv[3, pl.ds(half * HALF, HALF)].astype(F32)
        x = x + rrecv[1, 1 - half].astype(F32)
        acc[pl.ds(half * 2, 2)] = x.reshape(2, 64, D)

    def finish_rows(chunk, part):
        got = rrecv[2, chunk // 2, pl.ds((chunk % 2) * 64 + part * 32, 32)]
        return acc[chunk, pl.ds(part * 32, 32)] + got.astype(F32)

    odd = sec % 2
    steps = [1 + 2 * odd, 2, 3 - 2 * odd]
    secs = [
        [rcopy(SEC + 2 * i + n, xsend.at[i, n], xrecv.at[i, n], sdev(k)) for n in range(2)]
        for i, k in enumerate(steps)
    ]
    sides = [1 - xh, xh]

    def send_chunks(pairings):
        for n in range(2):
            for i in pairings:
                xsend[i, n] = finish_rows((sec + steps[i]) % 4, sides[n]).astype(BF16)
                secs[i][n].start()

    def own_rows(n):
        total = finish_rows(sec, sides[n])
        for i in range(3):
            total = total + xrecv[i, n].astype(F32)
        return total

    def counts_on():
        for c in cnt_p:
            c.wait_recv()
        cs2[...] = cs1[...] + cr2[0] + cr2[1] + cr2[2]
        for c in cnt_s:
            c.start()

    group = [sdev(1), sdev(2), sdev(3), xdev, sxdev(1), sxdev(2), sxdev(3)]
    cnt_s = [rcopy(CNT_S + k, cs2, cr3.at[k], dev) for k, dev in enumerate(group)]

    def match(o):
        h = hb[o]
        hf = h.astype(F32)
        sq = hf * hf
        part = sq[:, :128]
        for c in range(1, D // 128):
            part = part + sq[:, c * 128:(c + 1) * 128]
        norm = jnp.concatenate(
            [jnp.sum(part[i * 128:(i + 1) * 128].T, axis=0, keepdims=True) for i in range(HEADS // 128)],
            axis=1,
        )
        q = qs[pl.ds(o * TILE, TILE), :]
        s = nt_dot(q, h) * C1 - norm * C2
        p = jnp.exp2(s - jnp.max(s, axis=1, keepdims=True))
        weights = (p / jnp.sum(p, axis=1, keepdims=True)).astype(BF16)
        r = (q.astype(F32) - nn_dot(weights, h)).astype(BF16)
        rb[pl.ds(o * 2, 2)] = r.reshape(2, HALF, D)

    ring2[0][0].wait_recv()
    ring2[1][0].wait_recv()
    send_chunks((1, 0))
    ring2[0][1].wait_recv()
    ring2[1][1].wait_recv()
    send_chunks((2,))
    counts_on()

    head1.wait_recv()
    head2.wait_recv()
    match(0)

    for i in range(3):
        secs[i][0].wait_recv()
    xlast[0] = own_rows(0).astype(BF16)
    last = rcopy(XHI, xlast.at[0], xlast.at[1], xdev)
    last.start()
    match(1)

    row = lax.broadcasted_iota(jnp.int32, (HALF, D), 0)
    for b in range(4):
        x = rb[slot[b]]
        resid[pl.ds(b * HALF, HALF), :] = jnp.where(row < blive[0, b], x, jnp.zeros_like(x))

    old_copy.wait()
    for i in range(3):
        secs[i][1].wait_recv()
    for c in cnt_s:
        c.wait_recv()
    counts = cs2[...]
    for k in range(7):
        counts = counts + cr3[k]
    cfin[...] = counts
    place = core * 1024 + prim * 256 + sec * 64 + xh * 32
    counts = jnp.broadcast_to(cfin[pl.ds(place // HALF, 1), :], (32, HALF))
    at = lax.broadcasted_iota(jnp.int32, (32, HALF), 0) + place % HALF
    hit = lax.broadcasted_iota(jnp.int32, (32, HALF), 1) == at
    count = jnp.sum(jnp.where(hit, counts, 0.0), axis=1, keepdims=True)
    total = own_rows(1) + old[...]
    last.wait_recv()
    newc[...] = (total + xlast[1].astype(F32)) / (count + 1.0)

    for c in [stat1, stat2, head1, head2, cnt_t, last]:
        c.wait_send()
    for c in twins + cnt_p + cnt_s + ring1:
        c.wait_send()
    for pair in ring0 + ring2 + secs:
        for c in pair:
            c.wait_send()


def hand_over(new, resid, new_out, resid_out, sems):
    copies = [
        pltpu.make_async_copy(new, new_out, sems.at[0]),
        pltpu.make_async_copy(resid, resid_out, sems.at[1]),
    ]
    for c in copies:
        c.start()
    for c in copies:
        c.wait()


def per_device(vectors, centroids, head_index, boundary_rows, block_owner, block_live):
    any_spec = pl.BlockSpec(memory_space=pl.ANY)
    vmem = pl.BlockSpec(memory_space=pltpu.VMEM)
    smem = pl.BlockSpec(memory_space=pltpu.SMEM)
    scratch = [
        pltpu.VMEM((NT, 4, 2, 32, D), F32),
        pltpu.VMEM((NJ, TILE, D), F32),
        pltpu.VMEM((NT, TILE, D), BF16),
        pltpu.VMEM((ROWS, D), BF16),
        pltpu.VMEM((D, TILE), BF16),
        pltpu.VMEM((D, TILE), BF16),
        pltpu.VMEM((D, TILE), BF16),
        pltpu.VMEM((NT, TILE, HALF), F32),
        pltpu.VMEM((NT, TILE, TILE), F32),
        pltpu.VMEM((NT, TILE, TILE), F32),
        pltpu.VMEM((NT, TILE, TILE), F32),
        pltpu.VMEM((NT, TILE, ROWS), BF16),
        pltpu.VMEM((16, HALF), F32),
        pltpu.VMEM((16, ROWS), BF16),
        pltpu.VMEM((TILE, ROWS), BF16),
        pltpu.VMEM((TILE, ROWS), BF16),
        pltpu.VMEM((16, HALF), F32),
        pltpu.VMEM((4, TILE, D), BF16),
        pltpu.VMEM((4, TILE, D), BF16),
        pltpu.VMEM((3, 2, HALF, D), BF16),
        pltpu.VMEM((3, 2, HALF, D), BF16),
        pltpu.VMEM((4, 64, D), F32),
        pltpu.VMEM((3, 2, 32, D), BF16),
        pltpu.VMEM((3, 2, 32, D), BF16),
        pltpu.VMEM((2, 32, D), BF16),
        pltpu.VMEM((16, HALF), F32),
        pltpu.VMEM((16, HALF), F32),
        pltpu.VMEM((16, HALF), F32),
        pltpu.VMEM((3, 16, HALF), F32),
        pltpu.VMEM((7, 16, HALF), F32),
        pltpu.VMEM((NJ, 2, 8, TILE), F32),
        pltpu.VMEM((NJ, 2, 8, TILE), F32),
        pltpu.VMEM((HEADS, ROWS), BF16),
        pltpu.VMEM((2, HEADS, D), BF16),
        pltpu.VMEM((HEADS, D), BF16),
        pltpu.VMEM((4, HALF, D), BF16),
        pltpu.VMEM((32, D), F32),
        pltpu.SemaphoreType.DMA((N_REMOTE,)),
        pltpu.SemaphoreType.DMA((N_REMOTE,)),
        pltpu.SemaphoreType.DMA((N_LOCAL,)),
    ]
    new, resid = pl.pallas_call(
        kernel,
        out_shape=(
            pltpu.VMEM((32, D), F32),
            pltpu.VMEM((HEADS, D), BF16),
        ),
        in_specs=[any_spec, any_spec, vmem, vmem, smem, smem],
        out_specs=(vmem, vmem),
        scratch_shapes=scratch,
        compiler_params=pltpu.CompilerParams(
            collective_id=0, has_side_effects=True, vmem_limit_bytes=60 * 1024 * 1024
        ),
    )(
        vectors,
        centroids.reshape(4, 4, 2, 2, 32, D),
        head_index,
        boundary_rows.reshape(1, HEADS),
        block_owner.reshape(1, 4),
        block_live.reshape(1, 4),
    )
    new, resid = pl.pallas_call(
        hand_over,
        out_shape=(
            jax.ShapeDtypeStruct((32, D), F32),
            jax.ShapeDtypeStruct((HEADS, D), BF16),
        ),
        in_specs=[vmem, vmem],
        out_specs=(any_spec, any_spec),
        scratch_shapes=[pltpu.SemaphoreType.DMA((2,))],
        compiler_params=pltpu.CompilerParams(vmem_limit_bytes=4 * 1024 * 1024),
    )(new, resid)
    return new[None], resid[None, None]


def solution(mesh):
    in_specs = (
        P("dp", None),
        P("cent", None),
        P("cent", None),
        P("dp", "cent", None),
        P("dp", "cent", None),
        P("dp", "cent", None),
    )
    out_specs = (P("cent", "dp", None), P("dp", "cent", None, None))
    return jax.shard_map(
        per_device, mesh=mesh, in_specs=in_specs, out_specs=out_specs, check_vma=False
    )
```

```python
import math

import jax
import jax.numpy as jnp
from jax import lax
from jax.experimental import pallas as pl
from jax.experimental.pallas import tpu as pltpu
from jax.sharding import PartitionSpec as P

MESH = pl.DeviceIdType.MESH
F32 = jnp.float32
BF16 = jnp.bfloat16

D = 768
TILE = 256
NT = 8
NJ = 8
AHEAD = 2
HALF = 128
ROWS = NJ * TILE
HEADS = 512

C1 = 0.1 * math.log2(math.e)
C2 = 0.05 * math.log2(math.e)

STAT = 0
HEAD = 2
TWIN = 4
RING0 = 8
RING1 = 12
RING2 = 14
CNT_T = 18
CNT_P = 19
CNT_S = 22
SEC = 29
XHI = 35
N_REMOTE = 36

L_CEN = 0
L_VEC = 8
L_OLD = 16
N_LOCAL = 17


def nt_dot(a, b):
    return lax.dot_general(a, b, (((1,), (1,)), ((), ())), preferred_element_type=F32)


def nn_dot(a, b):
    return jnp.dot(a, b, preferred_element_type=F32)


def kernel(
    vec, cen, hidx, brow, bown, blive,
    newc, resid,
    cst, qst, cb, qb, qt0, qt1, qt2, bias, s0, s1, s2, e, cfin, alpha, w0, w1, cnt,
    tsend, trecv, rsend, rrecv, acc, xsend, xrecv, xlast,
    cs1, cs2, cr1, cr2, cr3,
    ssend, srecv, pick, hb, qs, rb, old,
    ssem, rsem, lsem,
):
    dp = lax.axis_index("dp")
    ce = lax.axis_index("cent")
    core = dp % 2
    xh = (dp // 2) % 2
    y = (dp // 4) % 4
    z = dp // 16
    prim = z * (1 - core) + y * core
    sec = y * (1 - core) + z * core
    pst = 16 * (1 - core) + 4 * core
    sst = 4 * (1 - core) + 16 * core

    def pdev(k):
        return (dp + ((prim + k) % 4 - prim) * pst, ce)

    def sdev(k):
        return (dp + ((sec + k) % 4 - sec) * sst, ce)

    def sxdev(k):
        return (sdev(k)[0] + 2 - 4 * xh, ce)

    twin = (dp + 1 - 2 * core, ce)
    xdev = (dp + 2 - 4 * xh, ce)
    side1 = (dp, 1 - ce)
    side2 = (dp + 2 - 4 * xh, 1 - ce)

    barrier = pltpu.get_barrier_semaphore()
    peers = [pdev(1), pdev(2), pdev(3), sdev(1), sdev(2), sdev(3), sxdev(1), sxdev(2), sxdev(3)]
    peers += [twin, xdev, side1, side2]
    for peer in peers:
        pl.semaphore_signal(barrier, inc=1, device_id=peer, device_id_type=MESH)

    def rcopy(i, src, dst, dev):
        return pltpu.make_async_remote_copy(
            src_ref=src, dst_ref=dst, send_sem=ssem.at[i], recv_sem=rsem.at[i],
            device_id=dev, device_id_type=MESH,
        )

    def lcopy(i, src, dst):
        return pltpu.make_async_copy(src, dst, lsem.at[i])

    cen_copies = [lcopy(L_CEN + t, cen.at[t, :, :, 0], cst.at[t]) for t in range(4)]
    cen_copies += [lcopy(L_CEN + 4 + t, cen.at[:, t, :, 1], cst.at[4 + t]) for t in range(4)]
    vec_copies = [
        lcopy(L_VEC + j, vec.at[pl.ds(j * TILE, TILE)], qst.at[j]) for j in range(NJ)
    ]
    vec_copies[0].start()
    cen_copies[0].start()
    for j in range(1, AHEAD):
        vec_copies[j].start()
    for t in range(1, NT):
        cen_copies[t].start()
    for j in range(AHEAD, NJ):
        vec_copies[j].start()
    old_copy = lcopy(L_OLD, cen.at[z, y, xh, core], old)
    old_copy.start()

    def load_q(j, qt_ref):
        lcopy(L_VEC + j, vec.at[pl.ds(j * TILE, TILE)], qst.at[j]).wait()
        x = qst[j].astype(BF16)
        qb[pl.ds(pl.multiple_of(j * TILE, TILE), TILE), :] = x
        qt_ref[...] = x.T

    def load_c(t):
        cen_copies[t].wait()
        x = cst[t].reshape(TILE, D).astype(BF16)
        cb[t] = x
        xf = x.astype(F32)
        norm = jnp.sum(xf * xf, axis=1, keepdims=True) * C2
        bias[t] = jnp.broadcast_to(norm, (TILE, HALF))

    def score(t, qt_ref, s_ref, top):
        b = bias[t]
        s = nn_dot(cb[t], qt_ref[...]) * C1 - jnp.concatenate([b, b], axis=1)
        s_ref[t] = s
        return jnp.maximum(top, jnp.max(s.reshape(TILE // 8, 8, TILE), axis=0))

    def expo(t, j, s_ref, top, total):
        p = jnp.exp2(s_ref[t].reshape(TILE // 8, 8, TILE) - top[None])
        e[t, :, pl.ds(pl.multiple_of(j * TILE, TILE), TILE)] = p.reshape(TILE, TILE).astype(BF16)
        return total + jnp.sum(p, axis=0)

    low = jnp.full((8, TILE), -jnp.inf, F32)
    zero = jnp.zeros((8, TILE), F32)

    def whole_max(x):
        return jnp.broadcast_to(jnp.max(x, axis=0, keepdims=True), x.shape)

    def whole_sum(x):
        return jnp.broadcast_to(jnp.sum(x, axis=0, keepdims=True), x.shape)

    def put_stats(j, top, total):
        ssend[j, 0] = top
        ssend[j, 1] = whole_sum(total)

    load_q(0, qt0)
    load_c(0)
    top0, top1 = low, low
    for t in range(NT):
        if t == 0:
            load_q(1, qt1)
        else:
            top1 = score(t - 1, qt1, s1, top1)
        if t + 1 < NT:
            load_c(t + 1)
        top0 = score(t, qt0, s0, top0)
    load_q(2, qt2)
    top1 = score(NT - 1, qt1, s1, top1)

    def both(j, s_next, qt_ref, qt_next, prevs):
        if qt_next is not None:
            load_q(j + 1, qt_next)
        new_top = low
        totals = [zero] * len(prevs)
        for t in range(NT):
            new_top = score(t, qt_ref, s_next, new_top)
            totals = [expo(t, i, ref, top, total) for (i, ref, top), total in zip(prevs, totals)]
        for (i, _, top), total in zip(prevs, totals):
            put_stats(i, top, total)
        return whole_max(new_top)

    top = both(2, s2, qt2, qt0, [(0, s0, whole_max(top0)), (1, s1, whole_max(top1))])

    def pair(i, top):
        j = 2 * i + 3
        top = both(j, s0, qt0, qt2, [(j - 1, s2, top)])
        return both(j + 1, s2, qt2, qt0, [(j, s0, top)])

    top = lax.fori_loop(0, 2, pair, top)
    top = both(7, s0, qt0, None, [(6, s2, top)])
    s_last = s0

    pl.semaphore_wait(barrier, len(peers))
    stat1 = rcopy(STAT, ssend.at[pl.ds(0, 7)], srecv.at[pl.ds(0, 7)], side1)
    stat1.start()
    total = zero
    for t in range(NT):
        total = expo(t, 7, s_last, top, total)
    put_stats(7, top, total)
    stat2 = rcopy(STAT + 1, ssend.at[pl.ds(7, 1)], srecv.at[pl.ds(7, 1)], side1)
    stat2.start()

    lane = lax.broadcasted_iota(jnp.int32, (HALF, HALF), 1)

    def unit_rows(ids, place):
        column = jnp.broadcast_to(ids.astype(F32), (HALF, HALF)).T
        for k in range(ROWS // HALF):
            yield column, k

    def pick_rows(ids, place, stored_id):
        for column, k in unit_rows(ids, place):
            hit = jnp.where(column == stored_id(k).astype(F32), 1.0, 0.0)
            pick[pl.ds(place * HALF, HALF), pl.ds(k * HALF, HALF)] = hit.astype(BF16)

    def centre_id(k):
        tile, part = k // 2, k % 2
        outer = part * 2 + lane // 64
        inner = lane % 64
        inner = (inner // 32) * 64 + inner % 32
        if tile < 4:
            return tile * 512 + outer * 128 + inner
        return outer * 512 + (tile - 4) * 128 + 32 + inner

    for place in range(4):
        pick_rows(hidx[:, pl.ds(place * HALF, HALF)], place, centre_id)
    heads = nn_dot(pick[...], cb[...].reshape(ROWS, D))
    hb[ce] = heads.astype(BF16)
    head1 = rcopy(HEAD, hb.at[ce, pl.ds(0, 256)], hb.at[ce, pl.ds(0, 256)], side1)
    head2 = rcopy(HEAD + 1, hb.at[ce, pl.ds(256, 256)], hb.at[ce, pl.ds(256, 256)], side2)
    head1.start()
    head2.start()

    def parts(base, place, step):
        if step == 0:
            t = base + (place + 2) % 4
            return (t, 0), (t, 1)
        if step == 1:
            return (base + (place + 1) % 4, 1), (base + (place + 3) % 4, 0)
        if step == 2:
            return (base + (place + 1) % 4, 0), (base + (place + 3) % 4, 1)
        return (base + place, 0), (base + place, 1)

    def tile_of(who, step):
        if who == 0:
            return parts((1 - core) * 4, sec, step)
        return parts(core * 4, prim, step)

    def scale(who, step, w_ref, columns, counts, last):
        out = []
        for side, (t, half) in enumerate(tile_of(who, step)):
            partial = []
            for c in columns:
                x = e[t, pl.ds(half * HALF, HALF), pl.ds(c * TILE, TILE)]
                x = x.reshape(HALF // 16, 16, TILE) * alpha[:, pl.ds(c * TILE, TILE)][None]
                x = x.reshape(HALF, TILE)
                w_ref[pl.ds(side * HALF, HALF), pl.ds(c * TILE, TILE)] = x
                partial.append(x[:, :HALF] + x[:, HALF:])
            count = counts[side]
            while partial:
                some, partial = partial[:4], partial[4:]
                while len(some) > 1:
                    some = [some[0] + some[1]] + some[2:] if len(some) != 4 else [some[0] + some[1], some[2] + some[3]]
                count = count + some[0].astype(F32)
            if last:
                cnt[pl.ds(t * 2 + half, 1), :] = jnp.sum(count.T, axis=0, keepdims=True)
            out.append(count)
        return out

    none = [jnp.zeros((HALF, HALF), F32)] * 2

    def row_scale(j):
        m1, l1, m2, l2 = ssend[j, 0], ssend[j, 1], srecv[j, 0], srecv[j, 1]
        m = jnp.maximum(m1, m2)
        f1 = jnp.exp2(m1 - m)
        a = f1 / (l1 * f1 + l2 * jnp.exp2(m2 - m))
        alpha[:, pl.ds(j * TILE, TILE)] = jnp.concatenate([a, a], axis=0).astype(BF16)

    order = [(0, 0), (0, 1), (1, 0), (0, 2), (1, 1), (1, 2), (0, 3), (1, 3)]
    w_refs = (w0, w1)

    early = (NJ - 1) * TILE
    stat1.wait_recv()
    for j in range(NJ - 1):
        row_scale(j)
    counted = [scale(*order[n], w_refs[n], range(NJ - 1), none, False) for n in range(2)]
    cst[4] = nn_dot(w0[:, pl.ds(0, early)], qb[pl.ds(0, early), :]).reshape(4, 2, 32, D)
    stat2.wait_recv()
    row_scale(NJ - 1)
    for n in range(2):
        scale(*order[n], w_refs[n], [NJ - 1], counted[n], True)

    twins = [rcopy(TWIN + s, tsend.at[s], trecv.at[s], twin) for s in range(4)]
    lead = [sec % 2 + (1 - 2 * (sec % 2)) * (k * (sec // 2) + (1 - k) * (1 - sec // 2)) for k in range(2)]
    chunks = [(lead[k], 1 - lead[k]) for k in range(2)]
    spots = [[pl.ds(pl.multiple_of(c * 64, 64), 64) for c in chunks[k]] for k in range(2)]
    around = [pdev(1), pdev(3)]

    def ring_parts(first, s):
        return [
            [
                rcopy(first + 2 * k + n, rsend.at[s, k, spots[k][n]], rrecv.at[s, k, spots[k][n]], around[k])
                for n in range(2)
            ]
            for k in range(2)
        ]

    ring0, ring2 = ring_parts(RING0, 0), ring_parts(RING2, 2)
    ring1 = [rcopy(RING1 + k, rsend.at[1, k], rrecv.at[1, k], around[k]) for k in range(2)]

    def own(s, half):
        return cst[s, pl.ds(half * 2, 2)].reshape(HALF, D)

    def send_part(s, n):
        for k in range(2):
            c = 2 * k + chunks[k][n]
            x = cst[s, c].reshape(64, D)
            x = x + trecv[s, pl.ds(pl.multiple_of(c * 64, 64), 64)].astype(F32)
            if s == 2:
                ring0[k][n].wait_recv()
                x = x + rrecv[0, k, spots[k][n]].astype(F32)
            rsend[s, k, spots[k][n]] = x.astype(BF16)
            (ring2 if s == 2 else ring0)[k][n].start()

    def send_middle():
        for k in range(2):
            x = own(1, k) + trecv[1, pl.ds(k * HALF, HALF)].astype(F32)
            rsend[1, k] = x.astype(BF16)
            ring1[k].start()

    cnt_t = rcopy(CNT_T, cnt, cr1, twin)
    for n, (who, step) in enumerate(order):
        if n == 0:
            out = nn_dot(w0[:, pl.ds(early, TILE)], qb[pl.ds(early, TILE), :])
            out = out + cst[4].reshape(TILE, D)
        else:
            out = nn_dot(w_refs[n % 2][...], qb[...])
        if 0 < n < len(order) - 1:
            scale(*order[n + 1], w_refs[(n + 1) % 2], range(NJ), none, True)
        if who == 0:
            tsend[step] = out.astype(BF16)
            twins[step].start()
            if step == 3:
                cnt_t.start()
                twins[2].wait_recv()
                send_part(2, 0)
        else:
            cst[step] = out.reshape(4, 2, 32, D)
            if step == 0:
                twins[0].wait_recv()
                send_part(0, 0)
                send_part(0, 1)
            if step == 1:
                twins[1].wait_recv()
                send_middle()
            if step == 3:
                send_part(2, 1)

    cnt_t.wait_recv()
    cs1[...] = cnt[...] + cr1[...]
    cnt_p = [rcopy(CNT_P + k, cs1, cr2.at[k], pdev(k + 1)) for k in range(3)]
    for c in cnt_p:
        c.start()

    owner = [bown[0, b] for b in range(4)]
    slot = []
    for b in range(4):
        earlier = jnp.int32(0)
        for other in range(b):
            earlier = earlier + jnp.where(owner[other] == owner[b], 1, 0)
        slot.append(owner[b] * 2 + earlier)
    for place in range(4):
        ids = jnp.zeros((1, HALF), jnp.int32)
        for b in range(4):
            here = jnp.where(slot[b] == place, 1, 0)
            ids = ids + brow[:, pl.ds(b * HALF, HALF)] * here
        pick_rows(ids, place, lambda k: lane + k * HALF)
    qs[...] = nn_dot(pick[...], qb[...]).astype(BF16)

    twins[3].wait_recv()
    ring1[0].wait_recv()
    ring1[1].wait_recv()
    for half in range(2):
        x = own(3, half) + trecv[3, pl.ds(half * HALF, HALF)].astype(F32)
        x = x + rrecv[1, 1 - half].astype(F32)
        acc[pl.ds(half * 2, 2)] = x.reshape(2, 64, D)

    def finish_rows(chunk, part):
        got = rrecv[2, chunk // 2, pl.ds((chunk % 2) * 64 + part * 32, 32)]
        return acc[chunk, pl.ds(part * 32, 32)] + got.astype(F32)

    odd = sec % 2
    steps = [1 + 2 * odd, 2, 3 - 2 * odd]
    secs = [
        [rcopy(SEC + 2 * i + n, xsend.at[i, n], xrecv.at[i, n], sdev(k)) for n in range(2)]
        for i, k in enumerate(steps)
    ]
    sides = [1 - xh, xh]

    def send_chunks(pairings):
        for n in range(2):
            for i in pairings:
                xsend[i, n] = finish_rows((sec + steps[i]) % 4, sides[n]).astype(BF16)
                secs[i][n].start()

    def own_rows(n):
        total = finish_rows(sec, sides[n])
        for i in range(3):
            total = total + xrecv[i, n].astype(F32)
        return total

    def counts_on():
        for c in cnt_p:
            c.wait_recv()
        cs2[...] = cs1[...] + cr2[0] + cr2[1] + cr2[2]
        for c in cnt_s:
            c.start()

    group = [sdev(1), sdev(2), sdev(3), xdev, sxdev(1), sxdev(2), sxdev(3)]
    cnt_s = [rcopy(CNT_S + k, cs2, cr3.at[k], dev) for k, dev in enumerate(group)]

    def match(o):
        h = hb[o]
        hf = h.astype(F32)
        sq = hf * hf
        part = sq[:, :128]
        for c in range(1, D // 128):
            part = part + sq[:, c * 128:(c + 1) * 128]
        norm = jnp.concatenate(
            [jnp.sum(part[i * 128:(i + 1) * 128].T, axis=0, keepdims=True) for i in range(HEADS // 128)],
            axis=1,
        )
        q = qs[pl.ds(o * TILE, TILE), :]
        s = nt_dot(q, h) * C1 - norm * C2
        p = jnp.exp2(s - jnp.max(s, axis=1, keepdims=True))
        weights = (p / jnp.sum(p, axis=1, keepdims=True)).astype(BF16)
        r = (q.astype(F32) - nn_dot(weights, h)).astype(BF16)
        rb[pl.ds(o * 2, 2)] = r.reshape(2, HALF, D)

    ring2[0][0].wait_recv()
    ring2[1][0].wait_recv()
    send_chunks((1, 0))
    ring2[0][1].wait_recv()
    ring2[1][1].wait_recv()
    send_chunks((2,))
    counts_on()

    head1.wait_recv()
    head2.wait_recv()
    match(0)

    for i in range(3):
        secs[i][0].wait_recv()
    xlast[0] = own_rows(0).astype(BF16)
    last = rcopy(XHI, xlast.at[0], xlast.at[1], xdev)
    last.start()
    match(1)

    row = lax.broadcasted_iota(jnp.int32, (HALF, D), 0)
    for b in range(4):
        x = rb[slot[b]]
        resid[pl.ds(b * HALF, HALF), :] = jnp.where(row < blive[0, b], x, jnp.zeros_like(x))

    old_copy.wait()
    for i in range(3):
        secs[i][1].wait_recv()
    for c in cnt_s:
        c.wait_recv()
    counts = cs2[...]
    for k in range(7):
        counts = counts + cr3[k]
    cfin[...] = counts
    place = core * 1024 + prim * 256 + sec * 64 + xh * 32
    counts = jnp.broadcast_to(cfin[pl.ds(place // HALF, 1), :], (32, HALF))
    at = lax.broadcasted_iota(jnp.int32, (32, HALF), 0) + place % HALF
    hit = lax.broadcasted_iota(jnp.int32, (32, HALF), 1) == at
    count = jnp.sum(jnp.where(hit, counts, 0.0), axis=1, keepdims=True)
    total = own_rows(1) + old[...]
    last.wait_recv()
    newc[...] = (total + xlast[1].astype(F32)) / (count + 1.0)

    for c in [stat1, stat2, head1, head2, cnt_t, last]:
        c.wait_send()
    for c in twins + cnt_p + cnt_s + ring1:
        c.wait_send()
    for pair in ring0 + ring2 + secs:
        for c in pair:
            c.wait_send()


def hand_over(new, resid, new_out, resid_out, sems):
    copies = [
        pltpu.make_async_copy(new, new_out, sems.at[0]),
        pltpu.make_async_copy(resid, resid_out, sems.at[1]),
    ]
    for c in copies:
        c.start()
    for c in copies:
        c.wait()


def per_device(vectors, centroids, head_index, boundary_rows, block_owner, block_live):
    any_spec = pl.BlockSpec(memory_space=pl.ANY)
    vmem = pl.BlockSpec(memory_space=pltpu.VMEM)
    smem = pl.BlockSpec(memory_space=pltpu.SMEM)
    scratch = [
        pltpu.VMEM((NT, 4, 2, 32, D), F32),
        pltpu.VMEM((NJ, TILE, D), F32),
        pltpu.VMEM((NT, TILE, D), BF16),
        pltpu.VMEM((ROWS, D), BF16),
        pltpu.VMEM((D, TILE), BF16),
        pltpu.VMEM((D, TILE), BF16),
        pltpu.VMEM((D, TILE), BF16),
        pltpu.VMEM((NT, TILE, HALF), F32),
        pltpu.VMEM((NT, TILE, TILE), F32),
        pltpu.VMEM((NT, TILE, TILE), F32),
        pltpu.VMEM((NT, TILE, TILE), F32),
        pltpu.VMEM((NT, TILE, ROWS), BF16),
        pltpu.VMEM((16, HALF), F32),
        pltpu.VMEM((16, ROWS), BF16),
        pltpu.VMEM((TILE, ROWS), BF16),
        pltpu.VMEM((TILE, ROWS), BF16),
        pltpu.VMEM((16, HALF), F32),
        pltpu.VMEM((4, TILE, D), BF16),
        pltpu.VMEM((4, TILE, D), BF16),
        pltpu.VMEM((3, 2, HALF, D), BF16),
        pltpu.VMEM((3, 2, HALF, D), BF16),
        pltpu.VMEM((4, 64, D), F32),
        pltpu.VMEM((3, 2, 32, D), BF16),
        pltpu.VMEM((3, 2, 32, D), BF16),
        pltpu.VMEM((2, 32, D), BF16),
        pltpu.VMEM((16, HALF), F32),
        pltpu.VMEM((16, HALF), F32),
        pltpu.VMEM((16, HALF), F32),
        pltpu.VMEM((3, 16, HALF), F32),
        pltpu.VMEM((7, 16, HALF), F32),
        pltpu.VMEM((NJ, 2, 8, TILE), F32),
        pltpu.VMEM((NJ, 2, 8, TILE), F32),
        pltpu.VMEM((HEADS, ROWS), BF16),
        pltpu.VMEM((2, HEADS, D), BF16),
        pltpu.VMEM((HEADS, D), BF16),
        pltpu.VMEM((4, HALF, D), BF16),
        pltpu.VMEM((32, D), F32),
        pltpu.SemaphoreType.DMA((N_REMOTE,)),
        pltpu.SemaphoreType.DMA((N_REMOTE,)),
        pltpu.SemaphoreType.DMA((N_LOCAL,)),
    ]
    new, resid = pl.pallas_call(
        kernel,
        out_shape=(
            pltpu.VMEM((32, D), F32),
            pltpu.VMEM((HEADS, D), BF16),
        ),
        in_specs=[any_spec, any_spec, vmem, vmem, smem, smem],
        out_specs=(vmem, vmem),
        scratch_shapes=scratch,
        compiler_params=pltpu.CompilerParams(
            collective_id=0, has_side_effects=True, vmem_limit_bytes=60 * 1024 * 1024
        ),
    )(
        vectors,
        centroids.reshape(4, 4, 2, 2, 32, D),
        head_index,
        boundary_rows.reshape(1, HEADS),
        block_owner.reshape(1, 4),
        block_live.reshape(1, 4),
    )
    new, resid = pl.pallas_call(
        hand_over,
        out_shape=(
            jax.ShapeDtypeStruct((32, D), F32),
            jax.ShapeDtypeStruct((HEADS, D), BF16),
        ),
        in_specs=[vmem, vmem],
        out_specs=(any_spec, any_spec),
        scratch_shapes=[pltpu.SemaphoreType.DMA((2,))],
        compiler_params=pltpu.CompilerParams(vmem_limit_bytes=4 * 1024 * 1024),
    )(new, resid)
    return new[None], resid[None, None]


def solution(mesh):
    in_specs = (
        P("dp", None),
        P("cent", None),
        P("cent", None),
        P("dp", "cent", None),
        P("dp", "cent", None),
        P("dp", "cent", None),
    )
    out_specs = (P("cent", "dp", None), P("dp", "cent", None, None))
    return jax.shard_map(
        per_device, mesh=mesh, in_specs=in_specs, out_specs=out_specs, check_vma=False
    )
```

```python
import math

import jax
import jax.numpy as jnp
from jax import lax
from jax.experimental import pallas as pl
from jax.experimental.pallas import tpu as pltpu
from jax.sharding import PartitionSpec as P

MESH = pl.DeviceIdType.MESH
F32 = jnp.float32
BF16 = jnp.bfloat16

D = 768
TILE = 256
NT = 8
NJ = 8
AHEAD = 2
HALF = 128
ROWS = NJ * TILE
HEADS = 512

C1 = 0.1 * math.log2(math.e)
C2 = 0.05 * math.log2(math.e)

STAT = 0
HEAD = 2
TWIN = 4
RING0 = 8
RING1 = 12
RING2 = 14
CNT_T = 18
CNT_P = 19
CNT_S = 22
SEC = 29
XHI = 35
N_REMOTE = 36

L_CEN = 0
L_VEC = 8
L_OLD = 16
N_LOCAL = 17


def nt_dot(a, b):
    return lax.dot_general(a, b, (((1,), (1,)), ((), ())), preferred_element_type=F32)


def nn_dot(a, b):
    return jnp.dot(a, b, preferred_element_type=F32)


def kernel(
    vec, cen, hidx, brow, bown, blive,
    newc, resid,
    cst, qst, cb, qb, qt0, qt1, qt2, bias, s0, s1, s2, e, cfin, alpha, w0, w1, cnt,
    tsend, trecv, rsend, rrecv, acc, xsend, xrecv, xlast,
    cs1, cs2, cr1, cr2, cr3,
    ssend, srecv, pick, hb, qs, rb, old,
    ssem, rsem, lsem,
):
    dp = lax.axis_index("dp")
    ce = lax.axis_index("cent")
    core = dp % 2
    xh = (dp // 2) % 2
    y = (dp // 4) % 4
    z = dp // 16
    prim = z * (1 - core) + y * core
    sec = y * (1 - core) + z * core
    pst = 16 * (1 - core) + 4 * core
    sst = 4 * (1 - core) + 16 * core

    def pdev(k):
        return (dp + ((prim + k) % 4 - prim) * pst, ce)

    def sdev(k):
        return (dp + ((sec + k) % 4 - sec) * sst, ce)

    def sxdev(k):
        return (sdev(k)[0] + 2 - 4 * xh, ce)

    twin = (dp + 1 - 2 * core, ce)
    xdev = (dp + 2 - 4 * xh, ce)
    side1 = (dp, 1 - ce)
    side2 = (dp + 2 - 4 * xh, 1 - ce)

    barrier = pltpu.get_barrier_semaphore()
    peers = [pdev(1), pdev(2), pdev(3), sdev(1), sdev(2), sdev(3), sxdev(1), sxdev(2), sxdev(3)]
    peers += [twin, xdev, side1, side2]
    for peer in peers:
        pl.semaphore_signal(barrier, inc=1, device_id=peer, device_id_type=MESH)

    def rcopy(i, src, dst, dev):
        return pltpu.make_async_remote_copy(
            src_ref=src, dst_ref=dst, send_sem=ssem.at[i], recv_sem=rsem.at[i],
            device_id=dev, device_id_type=MESH,
        )

    def lcopy(i, src, dst):
        return pltpu.make_async_copy(src, dst, lsem.at[i])

    cen_copies = [lcopy(L_CEN + t, cen.at[t, :, :, 0], cst.at[t]) for t in range(4)]
    cen_copies += [lcopy(L_CEN + 4 + t, cen.at[:, t, :, 1], cst.at[4 + t]) for t in range(4)]
    vec_copies = [
        lcopy(L_VEC + j, vec.at[pl.ds(j * TILE, TILE)], qst.at[j]) for j in range(NJ)
    ]
    vec_copies[0].start()
    cen_copies[0].start()
    for j in range(1, AHEAD):
        vec_copies[j].start()
    for t in range(1, NT):
        cen_copies[t].start()
    for j in range(AHEAD, NJ):
        vec_copies[j].start()
    old_copy = lcopy(L_OLD, cen.at[z, y, xh, core], old)
    old_copy.start()

    def load_q(j, qt_ref):
        lcopy(L_VEC + j, vec.at[pl.ds(j * TILE, TILE)], qst.at[j]).wait()
        x = qst[j].astype(BF16)
        qb[pl.ds(pl.multiple_of(j * TILE, TILE), TILE), :] = x
        qt_ref[...] = x.T

    def load_c(t):
        cen_copies[t].wait()
        x = cst[t].reshape(TILE, D).astype(BF16)
        cb[t] = x
        xf = x.astype(F32)
        norm = jnp.sum(xf * xf, axis=1, keepdims=True) * C2
        bias[t] = jnp.broadcast_to(norm, (TILE, HALF))

    def score(t, qt_ref, s_ref, top):
        b = bias[t]
        s = nn_dot(cb[t], qt_ref[...]) * C1 - jnp.concatenate([b, b], axis=1)
        s_ref[t] = s
        return jnp.maximum(top, jnp.max(s.reshape(TILE // 8, 8, TILE), axis=0))

    def expo(t, j, s_ref, top, total):
        p = jnp.exp2(s_ref[t].reshape(TILE // 8, 8, TILE) - top[None])
        e[t, :, pl.ds(pl.multiple_of(j * TILE, TILE), TILE)] = p.reshape(TILE, TILE).astype(BF16)
        return total + jnp.sum(p, axis=0)

    low = jnp.full((8, TILE), -jnp.inf, F32)
    zero = jnp.zeros((8, TILE), F32)

    def whole_max(x):
        return jnp.broadcast_to(jnp.max(x, axis=0, keepdims=True), x.shape)

    def whole_sum(x):
        return jnp.broadcast_to(jnp.sum(x, axis=0, keepdims=True), x.shape)

    def put_stats(j, top, total):
        ssend[j, 0] = top
        ssend[j, 1] = whole_sum(total)

    load_q(0, qt0)
    load_c(0)
    top0, top1 = low, low
    for t in range(NT):
        if t == 0:
            load_q(1, qt1)
        else:
            top1 = score(t - 1, qt1, s1, top1)
        if t + 1 < NT:
            load_c(t + 1)
        top0 = score(t, qt0, s0, top0)
    load_q(2, qt2)
    top1 = score(NT - 1, qt1, s1, top1)

    def both(j, s_next, qt_ref, qt_next, prevs):
        if qt_next is not None:
            load_q(j + 1, qt_next)
        new_top = low
        totals = [zero] * len(prevs)
        for t in range(NT):
            new_top = score(t, qt_ref, s_next, new_top)
            totals = [expo(t, i, ref, top, total) for (i, ref, top), total in zip(prevs, totals)]
        for (i, _, top), total in zip(prevs, totals):
            put_stats(i, top, total)
        return whole_max(new_top)

    top = both(2, s2, qt2, qt0, [(0, s0, whole_max(top0)), (1, s1, whole_max(top1))])

    def pair(i, top):
        j = 2 * i + 3
        top = both(j, s0, qt0, qt2, [(j - 1, s2, top)])
        return both(j + 1, s2, qt2, qt0, [(j, s0, top)])

    for i in range(2):
        top = pair(i, top)
    top = both(7, s0, qt0, None, [(6, s2, top)])
    s_last = s0

    pl.semaphore_wait(barrier, len(peers))
    stat1 = rcopy(STAT, ssend.at[pl.ds(0, 7)], srecv.at[pl.ds(0, 7)], side1)
    stat1.start()
    total = zero
    for t in range(NT):
        total = expo(t, 7, s_last, top, total)
    put_stats(7, top, total)
    stat2 = rcopy(STAT + 1, ssend.at[pl.ds(7, 1)], srecv.at[pl.ds(7, 1)], side1)
    stat2.start()

    lane = lax.broadcasted_iota(jnp.int32, (HALF, HALF), 1)

    def unit_rows(ids, place):
        column = jnp.broadcast_to(ids.astype(F32), (HALF, HALF)).T
        for k in range(ROWS // HALF):
            yield column, k

    def pick_rows(ids, place, stored_id):
        for column, k in unit_rows(ids, place):
            hit = jnp.where(column == stored_id(k).astype(F32), 1.0, 0.0)
            pick[pl.ds(place * HALF, HALF), pl.ds(k * HALF, HALF)] = hit.astype(BF16)

    def centre_id(k):
        tile, part = k // 2, k % 2
        outer = part * 2 + lane // 64
        inner = lane % 64
        inner = (inner // 32) * 64 + inner % 32
        if tile < 4:
            return tile * 512 + outer * 128 + inner
        return outer * 512 + (tile - 4) * 128 + 32 + inner

    for place in range(4):
        pick_rows(hidx[:, pl.ds(place * HALF, HALF)], place, centre_id)
    heads = nn_dot(pick[...], cb[...].reshape(ROWS, D))
    hb[ce] = heads.astype(BF16)
    head1 = rcopy(HEAD, hb.at[ce, pl.ds(0, 256)], hb.at[ce, pl.ds(0, 256)], side1)
    head2 = rcopy(HEAD + 1, hb.at[ce, pl.ds(256, 256)], hb.at[ce, pl.ds(256, 256)], side2)
    head1.start()
    head2.start()

    def parts(base, place, step):
        if step == 0:
            t = base + (place + 2) % 4
            return (t, 0), (t, 1)
        if step == 1:
            return (base + (place + 1) % 4, 1), (base + (place + 3) % 4, 0)
        if step == 2:
            return (base + (place + 1) % 4, 0), (base + (place + 3) % 4, 1)
        return (base + place, 0), (base + place, 1)

    def tile_of(who, step):
        if who == 0:
            return parts((1 - core) * 4, sec, step)
        return parts(core * 4, prim, step)

    def scale(who, step, w_ref, columns, counts, last):
        out = []
        for side, (t, half) in enumerate(tile_of(who, step)):
            partial = []
            for c in columns:
                x = e[t, pl.ds(half * HALF, HALF), pl.ds(c * TILE, TILE)]
                x = x.reshape(HALF // 16, 16, TILE) * alpha[:, pl.ds(c * TILE, TILE)][None]
                x = x.reshape(HALF, TILE)
                w_ref[pl.ds(side * HALF, HALF), pl.ds(c * TILE, TILE)] = x
                partial.append(x[:, :HALF] + x[:, HALF:])
            count = counts[side]
            while partial:
                some, partial = partial[:4], partial[4:]
                while len(some) > 1:
                    some = [some[0] + some[1]] + some[2:] if len(some) != 4 else [some[0] + some[1], some[2] + some[3]]
                count = count + some[0].astype(F32)
            if last:
                cnt[pl.ds(t * 2 + half, 1), :] = jnp.sum(count.T, axis=0, keepdims=True)
            out.append(count)
        return out

    none = [jnp.zeros((HALF, HALF), F32)] * 2

    def row_scale(j):
        m1, l1, m2, l2 = ssend[j, 0], ssend[j, 1], srecv[j, 0], srecv[j, 1]
        m = jnp.maximum(m1, m2)
        f1 = jnp.exp2(m1 - m)
        a = f1 / (l1 * f1 + l2 * jnp.exp2(m2 - m))
        alpha[:, pl.ds(j * TILE, TILE)] = jnp.concatenate([a, a], axis=0).astype(BF16)

    stat1.wait_recv()
    for j in range(NJ - 1):
        row_scale(j)
    first = scale(0, 0, w0, range(NJ - 1), none, False)
    stat2.wait_recv()
    row_scale(NJ - 1)
    scale(0, 0, w0, [NJ - 1], first, True)

    order = [(0, 0), (0, 1), (1, 0), (0, 2), (1, 1), (1, 2), (0, 3), (1, 3)]
    w_refs = (w0, w1)
    twins = [rcopy(TWIN + s, tsend.at[s], trecv.at[s], twin) for s in range(4)]
    lead = [sec % 2 + (1 - 2 * (sec % 2)) * (k * (sec // 2) + (1 - k) * (1 - sec // 2)) for k in range(2)]
    chunks = [(lead[k], 1 - lead[k]) for k in range(2)]
    spots = [[pl.ds(pl.multiple_of(c * 64, 64), 64) for c in chunks[k]] for k in range(2)]
    around = [pdev(1), pdev(3)]

    def ring_parts(first, s):
        return [
            [
                rcopy(first + 2 * k + n, rsend.at[s, k, spots[k][n]], rrecv.at[s, k, spots[k][n]], around[k])
                for n in range(2)
            ]
            for k in range(2)
        ]

    ring0, ring2 = ring_parts(RING0, 0), ring_parts(RING2, 2)
    ring1 = [rcopy(RING1 + k, rsend.at[1, k], rrecv.at[1, k], around[k]) for k in range(2)]

    def own(s, half):
        return cst[s, pl.ds(half * 2, 2)].reshape(HALF, D)

    def send_part(s, n):
        for k in range(2):
            c = 2 * k + chunks[k][n]
            x = cst[s, c].reshape(64, D)
            x = x + trecv[s, pl.ds(pl.multiple_of(c * 64, 64), 64)].astype(F32)
            if s == 2:
                ring0[k][n].wait_recv()
                x = x + rrecv[0, k, spots[k][n]].astype(F32)
            rsend[s, k, spots[k][n]] = x.astype(BF16)
            (ring2 if s == 2 else ring0)[k][n].start()

    def send_middle():
        for k in range(2):
            x = own(1, k) + trecv[1, pl.ds(k * HALF, HALF)].astype(F32)
            rsend[1, k] = x.astype(BF16)
            ring1[k].start()

    cnt_t = rcopy(CNT_T, cnt, cr1, twin)
    for n, (who, step) in enumerate(order):
        out = nn_dot(w_refs[n % 2][...], qb[...])
        if n + 1 < len(order):
            scale(*order[n + 1], w_refs[(n + 1) % 2], range(NJ), none, True)
        if who == 0:
            tsend[step] = out.astype(BF16)
            twins[step].start()
            if step == 3:
                cnt_t.start()
                twins[2].wait_recv()
                send_part(2, 0)
        else:
            cst[step] = out.reshape(4, 2, 32, D)
            if step == 0:
                twins[0].wait_recv()
                send_part(0, 0)
                send_part(0, 1)
            if step == 1:
                twins[1].wait_recv()
                send_middle()
            if step == 3:
                send_part(2, 1)

    cnt_t.wait_recv()
    cs1[...] = cnt[...] + cr1[...]
    cnt_p = [rcopy(CNT_P + k, cs1, cr2.at[k], pdev(k + 1)) for k in range(3)]
    for c in cnt_p:
        c.start()

    owner = [bown[0, b] for b in range(4)]
    slot = []
    for b in range(4):
        earlier = jnp.int32(0)
        for other in range(b):
            earlier = earlier + jnp.where(owner[other] == owner[b], 1, 0)
        slot.append(owner[b] * 2 + earlier)
    for place in range(4):
        ids = jnp.zeros((1, HALF), jnp.int32)
        for b in range(4):
            here = jnp.where(slot[b] == place, 1, 0)
            ids = ids + brow[:, pl.ds(b * HALF, HALF)] * here
        pick_rows(ids, place, lambda k: lane + k * HALF)
    qs[...] = nn_dot(pick[...], qb[...]).astype(BF16)

    twins[3].wait_recv()
    ring1[0].wait_recv()
    ring1[1].wait_recv()
    for half in range(2):
        x = own(3, half) + trecv[3, pl.ds(half * HALF, HALF)].astype(F32)
        x = x + rrecv[1, 1 - half].astype(F32)
        acc[pl.ds(half * 2, 2)] = x.reshape(2, 64, D)

    def finish_rows(chunk, part):
        got = rrecv[2, chunk // 2, pl.ds((chunk % 2) * 64 + part * 32, 32)]
        return acc[chunk, pl.ds(part * 32, 32)] + got.astype(F32)

    odd = sec % 2
    steps = [1 + 2 * odd, 2, 3 - 2 * odd]
    secs = [
        [rcopy(SEC + 2 * i + n, xsend.at[i, n], xrecv.at[i, n], sdev(k)) for n in range(2)]
        for i, k in enumerate(steps)
    ]
    sides = [1 - xh, xh]

    def send_chunks(pairings):
        for n in range(2):
            for i in pairings:
                xsend[i, n] = finish_rows((sec + steps[i]) % 4, sides[n]).astype(BF16)
                secs[i][n].start()

    def own_rows(n):
        total = finish_rows(sec, sides[n])
        for i in range(3):
            total = total + xrecv[i, n].astype(F32)
        return total

    def counts_on():
        for c in cnt_p:
            c.wait_recv()
        cs2[...] = cs1[...] + cr2[0] + cr2[1] + cr2[2]
        for c in cnt_s:
            c.start()

    group = [sdev(1), sdev(2), sdev(3), xdev, sxdev(1), sxdev(2), sxdev(3)]
    cnt_s = [rcopy(CNT_S + k, cs2, cr3.at[k], dev) for k, dev in enumerate(group)]

    def match(o):
        h = hb[o]
        hf = h.astype(F32)
        sq = hf * hf
        part = sq[:, :128]
        for c in range(1, D // 128):
            part = part + sq[:, c * 128:(c + 1) * 128]
        norm = jnp.concatenate(
            [jnp.sum(part[i * 128:(i + 1) * 128].T, axis=0, keepdims=True) for i in range(HEADS // 128)],
            axis=1,
        )
        q = qs[pl.ds(o * TILE, TILE), :]
        s = nt_dot(q, h) * C1 - norm * C2
        p = jnp.exp2(s - jnp.max(s, axis=1, keepdims=True))
        weights = (p / jnp.sum(p, axis=1, keepdims=True)).astype(BF16)
        r = (q.astype(F32) - nn_dot(weights, h)).astype(BF16)
        rb[pl.ds(o * 2, 2)] = r.reshape(2, HALF, D)

    ring2[0][0].wait_recv()
    ring2[1][0].wait_recv()
    send_chunks((1, 0))
    ring2[0][1].wait_recv()
    ring2[1][1].wait_recv()
    send_chunks((2,))
    counts_on()

    head1.wait_recv()
    head2.wait_recv()
    match(0)

    for i in range(3):
        secs[i][0].wait_recv()
    xlast[0] = own_rows(0).astype(BF16)
    last = rcopy(XHI, xlast.at[0], xlast.at[1], xdev)
    last.start()
    match(1)

    row = lax.broadcasted_iota(jnp.int32, (HALF, D), 0)
    for b in range(4):
        x = rb[slot[b]]
        resid[pl.ds(b * HALF, HALF), :] = jnp.where(row < blive[0, b], x, jnp.zeros_like(x))

    old_copy.wait()
    for i in range(3):
        secs[i][1].wait_recv()
    for c in cnt_s:
        c.wait_recv()
    counts = cs2[...]
    for k in range(7):
        counts = counts + cr3[k]
    cfin[...] = counts
    place = core * 1024 + prim * 256 + sec * 64 + xh * 32
    counts = jnp.broadcast_to(cfin[pl.ds(place // HALF, 1), :], (32, HALF))
    at = lax.broadcasted_iota(jnp.int32, (32, HALF), 0) + place % HALF
    hit = lax.broadcasted_iota(jnp.int32, (32, HALF), 1) == at
    count = jnp.sum(jnp.where(hit, counts, 0.0), axis=1, keepdims=True)
    total = own_rows(1) + old[...]
    last.wait_recv()
    newc[...] = (total + xlast[1].astype(F32)) / (count + 1.0)

    for c in [stat1, stat2, head1, head2, cnt_t, last]:
        c.wait_send()
    for c in twins + cnt_p + cnt_s + ring1:
        c.wait_send()
    for pair in ring0 + ring2 + secs:
        for c in pair:
            c.wait_send()


def hand_over(new, resid, new_out, resid_out, sems):
    copies = [
        pltpu.make_async_copy(new, new_out, sems.at[0]),
        pltpu.make_async_copy(resid, resid_out, sems.at[1]),
    ]
    for c in copies:
        c.start()
    for c in copies:
        c.wait()


def per_device(vectors, centroids, head_index, boundary_rows, block_owner, block_live):
    any_spec = pl.BlockSpec(memory_space=pl.ANY)
    vmem = pl.BlockSpec(memory_space=pltpu.VMEM)
    smem = pl.BlockSpec(memory_space=pltpu.SMEM)
    scratch = [
        pltpu.VMEM((NT, 4, 2, 32, D), F32),
        pltpu.VMEM((NJ, TILE, D), F32),
        pltpu.VMEM((NT, TILE, D), BF16),
        pltpu.VMEM((ROWS, D), BF16),
        pltpu.VMEM((D, TILE), BF16),
        pltpu.VMEM((D, TILE), BF16),
        pltpu.VMEM((D, TILE), BF16),
        pltpu.VMEM((NT, TILE, HALF), F32),
        pltpu.VMEM((NT, TILE, TILE), F32),
        pltpu.VMEM((NT, TILE, TILE), F32),
        pltpu.VMEM((NT, TILE, TILE), F32),
        pltpu.VMEM((NT, TILE, ROWS), BF16),
        pltpu.VMEM((16, HALF), F32),
        pltpu.VMEM((16, ROWS), BF16),
        pltpu.VMEM((TILE, ROWS), BF16),
        pltpu.VMEM((TILE, ROWS), BF16),
        pltpu.VMEM((16, HALF), F32),
        pltpu.VMEM((4, TILE, D), BF16),
        pltpu.VMEM((4, TILE, D), BF16),
        pltpu.VMEM((3, 2, HALF, D), BF16),
        pltpu.VMEM((3, 2, HALF, D), BF16),
        pltpu.VMEM((4, 64, D), F32),
        pltpu.VMEM((3, 2, 32, D), BF16),
        pltpu.VMEM((3, 2, 32, D), BF16),
        pltpu.VMEM((2, 32, D), BF16),
        pltpu.VMEM((16, HALF), F32),
        pltpu.VMEM((16, HALF), F32),
        pltpu.VMEM((16, HALF), F32),
        pltpu.VMEM((3, 16, HALF), F32),
        pltpu.VMEM((7, 16, HALF), F32),
        pltpu.VMEM((NJ, 2, 8, TILE), F32),
        pltpu.VMEM((NJ, 2, 8, TILE), F32),
        pltpu.VMEM((HEADS, ROWS), BF16),
        pltpu.VMEM((2, HEADS, D), BF16),
        pltpu.VMEM((HEADS, D), BF16),
        pltpu.VMEM((4, HALF, D), BF16),
        pltpu.VMEM((32, D), F32),
        pltpu.SemaphoreType.DMA((N_REMOTE,)),
        pltpu.SemaphoreType.DMA((N_REMOTE,)),
        pltpu.SemaphoreType.DMA((N_LOCAL,)),
    ]
    new, resid = pl.pallas_call(
        kernel,
        out_shape=(
            pltpu.VMEM((32, D), F32),
            pltpu.VMEM((HEADS, D), BF16),
        ),
        in_specs=[any_spec, any_spec, vmem, vmem, smem, smem],
        out_specs=(vmem, vmem),
        scratch_shapes=scratch,
        compiler_params=pltpu.CompilerParams(
            collective_id=0, has_side_effects=True, vmem_limit_bytes=60 * 1024 * 1024
        ),
    )(
        vectors,
        centroids.reshape(4, 4, 2, 2, 32, D),
        head_index,
        boundary_rows.reshape(1, HEADS),
        block_owner.reshape(1, 4),
        block_live.reshape(1, 4),
    )
    new, resid = pl.pallas_call(
        hand_over,
        out_shape=(
            jax.ShapeDtypeStruct((32, D), F32),
            jax.ShapeDtypeStruct((HEADS, D), BF16),
        ),
        in_specs=[vmem, vmem],
        out_specs=(any_spec, any_spec),
        scratch_shapes=[pltpu.SemaphoreType.DMA((2,))],
        compiler_params=pltpu.CompilerParams(vmem_limit_bytes=4 * 1024 * 1024),
    )(new, resid)
    return new[None], resid[None, None]


def solution(mesh):
    in_specs = (
        P("dp", None),
        P("cent", None),
        P("cent", None),
        P("dp", "cent", None),
        P("dp", "cent", None),
        P("dp", "cent", None),
    )
    out_specs = (P("cent", "dp", None), P("dp", "cent", None, None))
    return jax.shard_map(
        per_device, mesh=mesh, in_specs=in_specs, out_specs=out_specs, check_vma=False
    )
```
